256 devices in a mesh: blk: 8 (over x_lo, y), group: 32 (over x_hi, z, core).
Axes of the slice: x: 4 (x_hi: 2, x_lo: 2; x = x_hi * 2 + x_lo), y: 4, z: 8, core: 2. Of those that a mesh axis runs over, the one named last changes fastest.
Arguments:
- trace_emb: bfloat16 [131072, 1152], P(('blk', 'group')), may hold values from -1 to 1
- code_emb: bfloat16 [2048, 1152], P(('blk', 'group')), may hold values from -1 to 1
- trace_ids: int32 [131072], P(('blk', 'group')), may hold values from 0 to 511
- code_ids: int32 [2048], P(('blk', 'group')), may hold values from 0 to 511
- log_scale: float32 [1], replicated, may hold values from 3.9 to 4.2
- bias: float32 [1], replicated, may hold values from -7.5 to -6
Outputs:
- trace_grad: bfloat16 [131072, 1152], P(('blk', 'group'))
- code_grad: bfloat16 [2048, 1152], P(('blk', 'group'))
The draws below stay inside these ranges and needn't reach their ends.
All inputs are finite; a program needn't handle non-finite values.
Results may differ from the reference program's by a relative error of at most 0.0044.
Values may be sent and summed in bfloat16 or wider, within the bound.
A program may use at most 128 MiB of HBM per device.

```python
import jax
import jax.numpy as jnp
from jax import lax

D = 1152
ROWS = 512
TRACES = 131072
CODES = 2048
N_GROUP = 32


def identity_rows(key):
    return jax.random.truncated_normal(jax.random.fold_in(key, 501), -4.0, 4.0, (CODES // 4, D), jnp.float32) * D ** (-0.5)


def sample_labels(key, salt, count):
    local = jax.random.fold_in(key, salt)
    first, second, third = jax.random.split(local, 3)
    labels = jax.random.randint(first, (count,), 0, CODES // 4, jnp.int32)
    low_at = jax.random.randint(second, (), 0, count, jnp.int32)
    offset = jax.random.randint(third, (), 1, count, jnp.int32)
    high_at = (low_at + offset) % count
    return labels.at[low_at].set(0).at[high_at].set(CODES // 4 - 1)


def mix_rows(table, labels, align, noise):
    rest = jnp.sqrt(1.0 - align * align)
    mixed = align * table[labels] + rest * noise
    return mixed.astype(jnp.bfloat16)


def draw_trace_ids(key, part):
    return sample_labels(key, 11, TRACES)


def draw_code_ids(key, part):
    return sample_labels(key, 12, CODES)


def draw_trace_emb(key, part):
    own_key = jax.random.fold_in(key, 3)
    table = identity_rows(key)
    labels = sample_labels(key, 11, TRACES)
    first, second = jax.random.split(own_key)
    align = jax.random.uniform(first, (TRACES, 1), jnp.float32, 0.25, 0.4)
    noise = jax.random.truncated_normal(second, -4.0, 4.0, (TRACES, D), jnp.float32) * D ** (-0.5)
    result = mix_rows(table, labels, align, noise)
    return result


def draw_code_emb(key, part):
    own_key = jax.random.fold_in(key, 4)
    table = identity_rows(key)
    labels = sample_labels(key, 12, CODES)
    first, second = jax.random.split(own_key)
    align = jax.random.uniform(first, (CODES, 1), jnp.float32, 0.25, 0.4)
    noise = jax.random.truncated_normal(second, -4.0, 4.0, (CODES, D), jnp.float32) * D ** (-0.5)
    result = mix_rows(table, labels, align, noise)
    return result


def setup_inputs(seed: int = 0) -> dict:
    arg_keys = jax.random.split(jax.random.key(seed), 7)
    return {
        "trace_emb": draw_trace_emb(jax.random.fold_in(arg_keys[6], 71), 0),
        "code_emb": draw_code_emb(jax.random.fold_in(arg_keys[6], 71), 0),
        "trace_ids": draw_trace_ids(jax.random.fold_in(arg_keys[6], 71), 0),
        "code_ids": draw_code_ids(jax.random.fold_in(arg_keys[6], 71), 0),
        "log_scale": jnp.clip(jax.random.uniform(arg_keys[4], (1,), jnp.float32, 3.9, 4.2), 3.9, 4.2),
        "bias": jnp.clip(jax.random.uniform(arg_keys[5], (1,), jnp.float32, -7.5, -6.0), -7.5, -6.0),
    }


def reference(trace_emb, code_emb, trace_ids, code_ids, log_scale, bias):
    scale = jnp.exp(log_scale[0])
    shift = bias[0]
    size = ROWS * N_GROUP
    count = TRACES // size
    blocks = trace_emb.reshape(count, size, D)
    labels = trace_ids.reshape(count, size)

    def visit(total, item):
        traces, marks = item
        logits = scale * jnp.dot(traces, code_emb.T, preferred_element_type=jnp.float32) + shift
        sign = jnp.where(marks[:, None] == code_ids[None, :], 1.0, -1.0).astype(jnp.float32)
        slope = (-scale * sign * jax.nn.sigmoid(-sign * logits)).astype(jnp.bfloat16)
        trace_part = jnp.dot(slope, code_emb, preferred_element_type=jnp.float32).astype(jnp.bfloat16)
        total = total + jnp.dot(slope.T, traces, preferred_element_type=jnp.float32)
        return total, trace_part

    start = jnp.zeros((CODES, D), jnp.float32)
    code_total, trace_parts = lax.scan(visit, start, (blocks, labels))
    return trace_parts.reshape(TRACES, D), code_total.astype(jnp.bfloat16)
```

```python
import jax
import jax.numpy as jnp
from jax import lax
from jax.experimental import pallas as pl
from jax.experimental.pallas import tpu as pltpu
from jax.sharding import PartitionSpec as P

MESH = pl.DeviceIdType.MESH
F32 = jnp.float32
BF16 = jnp.bfloat16

NY, NX, NZ = 4, 4, 8
SHARD = 8
WIDTH = 1152
ROWS = 512
A0, A1 = 0, 512
B0, B1 = 512, 1024
C0, C1 = 1024, 1152
WIDE = 1280
SPAN = NX * NZ * SHARD
PLANE = NY * SPAN


def place():
    blk = lax.axis_index("blk")
    group = lax.axis_index("group")
    x = (group // 16) * 2 + blk // 4
    return blk % 4, x, (group // 2) % NZ, group % 2


def device(y, x, z, core):
    return ((x % 2) * 4 + y, ((x // 2) * NZ + z) * 2 + core)


def remote(src, dst, sems, index, target):
    return pltpu.make_async_remote_copy(
        src_ref=src,
        dst_ref=dst,
        send_sem=sems[0].at[index],
        recv_sem=sems[1].at[index],
        device_id=target,
        device_id_type=MESH,
    )


def kernel(
    trace_ref, code_ref, tid_ref, cid_ref, scale_ref, shift_ref,
    trace_out, code_out,
    traces, tids, codes, flat, slopes, parts,
    recv_a1, recv_b1, recv_c1, sum_a, sum_b, sum_c, recv_a2, recv_b2, recv_c2,
    sum_ab, sum_c2, recv_ab3, recv_c3, tg_own, tg_send, tg_recv,
    s_d, r_d, s_ag, r_ag, s_rs, r_rs,
):
    y, x, z, core = place()
    ag = (s_ag, r_ag)
    rs = (s_rs, r_rs)
    dd = (s_d, r_d)

    def on_y(k):
        return device((y + k) % NY, x, z, core)

    def on_x(k):
        return device(y, (x + k) % NX, z, core)

    def on_z(k):
        return device(y, x, (z + k) % NZ, core)

    other = device(y, x, z, 1 - core)

    barrier = pltpu.get_barrier_semaphore()
    partners = [on_y(k) for k in (1, 2, 3)] + [on_x(k) for k in (1, 2, 3)]
    partners += [on_z(k) for k in range(1, NZ)] + [other]
    for partner in partners:
        pl.semaphore_signal(barrier, inc=1, device_id=partner, device_id_type=MESH)

    ids = cid_ref[...].astype(jnp.int32)
    high = (ids // 16).astype(F32)
    low = (ids % 16).astype(F32)
    lane = lax.broadcasted_iota(jnp.int32, (SHARD, 128), 1)
    tile = jnp.where(lane == 0, high, jnp.where(lane == 1, low, 0.0)).astype(BF16)
    codes[y, x, z, :, 0:WIDTH] = code_ref[...]
    codes[y, x, z, :, WIDTH:WIDE] = tile
    pl.semaphore_wait(barrier, len(partners))

    g1 = []
    for k in range(1, NZ):
        ref = codes.at[y, x, z, :, A0:B1]
        g1.append(remote(ref, ref, ag, k - 1, on_z(k)))
    g1c = []
    for k in range(1, NX):
        ref = codes.at[y, x, z, :, C0:WIDE]
        g1c.append(remote(ref, ref, ag, 6 + k, on_x(k)))
    for copy in g1 + g1c:
        copy.start()

    d1 = remote(trace_ref, traces.at[ROWS : 2 * ROWS], dd, 0, other)
    d2 = remote(tid_ref, tids.at[1], dd, 1, other)
    d1.start()
    d2.start()
    traces[0:ROWS] = trace_ref[...]
    tids[0] = tid_ref[...]

    g2 = []
    for copy in g1c:
        copy.wait_recv()
    for k in range(1, NY):
        ref = codes.at[y, :, z, :, C0:WIDE]
        g2.append(remote(ref, ref, ag, 9 + k, on_y(k)))
        g2[-1].start()
    g2c = list(g2)
    for copy in g1:
        copy.wait_recv()
    g2ab = []
    for k in range(1, 4):
        ref = codes.at[y, x, :, :, A0:A1]
        g2ab.append(remote(ref, ref, ag, 12 + k, on_x(k)))
        ref = codes.at[y, x, :, :, B0:B1]
        g2ab.append(remote(ref, ref, ag, 15 + k, on_y(k)))
    for copy in g2ab:
        copy.start()

    g3 = []
    for copy in g2c:
        copy.wait_recv()
    for k in range(1, NZ):
        ref = codes.at[:, :, z, :, C0:WIDE]
        g3.append(remote(ref, ref, ag, 18 + k, on_z(k)))
        g3[-1].start()
    for copy in g2ab:
        copy.wait_recv()
    for k in range(1, 4):
        ref = codes.at[y, :, :, :, A0:A1]
        g3.append(remote(ref, ref, ag, 25 + k, on_y(k)))
        g3[-1].start()
        ref = codes.at[:, x, :, :, B0:B1]
        g3.append(remote(ref, ref, ag, 28 + k, on_x(k)))
        g3[-1].start()
    d1.wait()
    d2.wait()
    for copy in g3:
        copy.wait_recv()

    scale = jnp.exp(scale_ref[...])
    shift = shift_ref[...]
    trace_ids = jnp.concatenate([tids[0], tids[1]], axis=1).astype(F32)

    def send_a1(j, q):
        return remote(
            parts.at[q, :, :, :, A0:A1], recv_a1.at[j - 1], rs, j - 1, on_y(j)
        )

    def send_b1(j, q, k):
        return remote(
            parts.at[q, (x + k) % NX, :, :, B0:B1], recv_b1.at[k - 1, q], rs, 3 + j * 3 + k - 1, on_x(k)
        )

    @pl.loop(0, NY)
    def _(step):
        j = (step + 1) % NY
        q = (y + j) % NY
        at = pl.multiple_of(q * SPAN, SPAN)
        for i in range(NX):
            block = codes[q, i, :, :, 0:WIDTH].astype(F32).reshape(NZ * SHARD, WIDTH)
            flat[pl.ds(at + i * NZ * SHARD, NZ * SHARD), :] = block.astype(BF16)
        marks = codes[q, :, :, :, WIDTH:WIDE].astype(F32).reshape(SPAN, 128)
        code_ids = marks[:, 0:1] * 16.0 + marks[:, 1:2]
        logits = lax.dot_general(
            flat[pl.ds(at, SPAN), :], traces[...], (((1,), (1,)), ((), ())), preferred_element_type=F32
        )
        logits = logits * scale + shift
        same = code_ids == trace_ids
        raised = jnp.exp(jnp.where(same, logits, -logits))
        slope = jnp.where(same, -scale, scale) / (1.0 + raised)
        slopes[pl.ds(at, SPAN), :] = slope.astype(BF16)
        grad = jnp.dot(slopes[pl.ds(at, SPAN), :], traces[...], preferred_element_type=F32)
        parts[q] = grad.reshape(NX, NZ, SHARD, WIDTH).astype(BF16)

        @pl.when(j != 0)
        def _():
            send_a1(j, q).start()

        for k in range(1, NX):
            send_b1(j, q, k).start()

    c1 = []
    for k in range(1, NZ):
        c1.append(
            remote(parts.at[:, :, (z + k) % NZ, :, C0:C1], recv_c1.at[k - 1], rs, 14 + k, on_z(k))
        )
        c1[-1].start()

    def trace_rows(first):
        return lax.dot_general(
            slopes[:, first : first + 256], flat[...], (((0,), (0,)), ((), ())), preferred_element_type=F32
        )

    for n in range(2):
        tg_send[n * 256 : n * 256 + 256, :] = trace_rows(ROWS + n * 256)
    d3 = remote(tg_send, tg_recv, dd, 2, other)
    d3.start()
    for n in range(2):
        tg_own[n * 256 : n * 256 + 256, :] = trace_rows(n * 256)

    for copy in c1:
        copy.wait_recv()
    for i in range(NY):
        total = parts[i, :, z, :, C0:C1].astype(F32)
        for k in range(NZ - 1):
            total = total + recv_c1[k, i].astype(F32)
        sum_c[i] = total.astype(BF16)
    c2 = []
    for k in range(1, NY):
        c2.append(remote(sum_c.at[(y + k) % NY], recv_c2.at[k - 1], rs, 21 + k, on_y(k)))
        c2[-1].start()

    for k in range(1, NX):
        for j in range(NY):
            send_b1(j, (y + j) % NY, k).wait_recv()
    for i in range(NY):
        total = parts[i, x, :, :, B0:B1].astype(F32)
        for k in range(NX - 1):
            total = total + recv_b1[k, i].astype(F32)
        sum_b[i] = total.astype(BF16)
    b2 = []
    for k in range(1, NY):
        b2.append(remote(sum_b.at[(y + k) % NY], recv_b2.at[k - 1], rs, 24 + k, on_y(k)))
        b2[-1].start()

    for j in range(1, NY):
        send_a1(j, (y + j) % NY).wait_recv()
    for i in range(NX):
        total = parts[y, i, :, :, A0:A1].astype(F32)
        for k in range(NY - 1):
            total = total + recv_a1[k, i].astype(F32)
        sum_a[i] = total.astype(BF16)
    a2 = []
    for k in range(1, NX):
        a2.append(remote(sum_a.at[(x + k) % NX], recv_a2.at[k - 1], rs, 27 + k, on_x(k)))
        a2[-1].start()

    for copy in c2:
        copy.wait_recv()
    total = sum_c[y].astype(F32)
    for k in range(NY - 1):
        total = total + recv_c2[k].astype(F32)
    sum_c2[...] = total.astype(BF16)
    c3 = []
    for k in range(1, NX):
        c3.append(remote(sum_c2.at[(x + k) % NX], recv_c3.at[k - 1], rs, 30 + k, on_x(k)))
        c3[-1].start()
    for copy in b2:
        copy.wait_recv()
    total = sum_b[y].astype(F32)
    for k in range(NY - 1):
        total = total + recv_b2[k].astype(F32)
    sum_ab[:, :, B0:B1] = total.astype(BF16)
    for copy in a2:
        copy.wait_recv()
    total = sum_a[x].astype(F32)
    for k in range(NX - 1):
        total = total + recv_a2[k].astype(F32)
    sum_ab[:, :, A0:A1] = total.astype(BF16)
    ab3 = []
    for k in range(1, NZ):
        ab3.append(remote(sum_ab.at[(z + k) % NZ], recv_ab3.at[k - 1], rs, 33 + k, on_z(k)))
        ab3[-1].start()

    d3.wait()
    trace_out[...] = (tg_own[...] + tg_recv[...]).astype(BF16)

    for copy in c3:
        copy.wait_recv()
    total = sum_c2[x].astype(F32)
    for k in range(NX - 1):
        total = total + recv_c3[k].astype(F32)
    code_out[:, C0:C1] = total.astype(BF16)
    for copy in ab3:
        copy.wait_recv()
    total = sum_ab[z].astype(F32)
    for k in range(NZ - 1):
        total = total + recv_ab3[k].astype(F32)
    code_out[:, A0:B1] = total.astype(BF16)

    for copy in g1 + g1c + g2c + g2ab + g3 + c1 + c2 + b2 + a2 + c3 + ab3:
        copy.wait_send()
    for j in range(NY):
        if j:
            send_a1(j, (y + j) % NY).wait_send()
        for k in range(1, NX):
            send_b1(j, (y + j) % NY, k).wait_send()


def per_device(trace_emb, code_emb, trace_ids, code_ids, log_scale, bias):
    vmem = pl.BlockSpec(memory_space=pltpu.VMEM)
    dma = pltpu.SemaphoreType.DMA
    scratch = [
        pltpu.VMEM((2 * ROWS, WIDTH), BF16),
        pltpu.VMEM((2, 1, ROWS), jnp.int32),
        pltpu.VMEM((NY, NX, NZ, SHARD, WIDE), BF16),
        pltpu.VMEM((PLANE, WIDTH), BF16),
        pltpu.VMEM((PLANE, 2 * ROWS), BF16),
        pltpu.VMEM((NY, NX, NZ, SHARD, WIDTH), BF16),
        pltpu.VMEM((NY - 1, NX, NZ, SHARD, A1 - A0), BF16),
        pltpu.VMEM((NX - 1, NY, NZ, SHARD, B1 - B0), BF16),
        pltpu.VMEM((NZ - 1, NY, NX, SHARD, C1 - C0), BF16),
        pltpu.VMEM((NX, NZ, SHARD, A1 - A0), BF16),
        pltpu.VMEM((NY, NZ, SHARD, B1 - B0), BF16),
        pltpu.VMEM((NY, NX, SHARD, C1 - C0), BF16),
        pltpu.VMEM((NX - 1, NZ, SHARD, A1 - A0), BF16),
        pltpu.VMEM((NY - 1, NZ, SHARD, B1 - B0), BF16),
        pltpu.VMEM((NY - 1, NX, SHARD, C1 - C0), BF16),
        pltpu.VMEM((NZ, SHARD, B1 - A0), BF16),
        pltpu.VMEM((NX, SHARD, C1 - C0), BF16),
        pltpu.VMEM((NZ - 1, SHARD, B1 - A0), BF16),
        pltpu.VMEM((NX - 1, SHARD, C1 - C0), BF16),
        pltpu.VMEM((ROWS, WIDTH), F32),
        pltpu.VMEM((ROWS, WIDTH), F32),
        pltpu.VMEM((ROWS, WIDTH), F32),
        dma((3,)),
        dma((3,)),
        dma((32,)),
        dma((32,)),
        dma((41,)),
        dma((41,)),
    ]
    return pl.pallas_call(
        kernel,
        out_shape=(
            jax.ShapeDtypeStruct((ROWS, WIDTH), BF16),
            jax.ShapeDtypeStruct((SHARD, WIDTH), BF16),
        ),
        in_specs=[vmem] * 6,
        out_specs=(vmem, vmem),
        scratch_shapes=scratch,
        compiler_params=pltpu.CompilerParams(
            collective_id=0, has_side_effects=True, vmem_limit_bytes=56 * 2**20
        ),
        name="contrast",
    )(
        trace_emb,
        code_emb,
        trace_ids.reshape(1, ROWS),
        code_ids.reshape(SHARD, 1),
        log_scale.reshape(1, 1),
        bias.reshape(1, 1),
    )


def solution(mesh):
    placed = (
        P(("blk", "group"), None),
        P(("blk", "group"), None),
        P(("blk", "group")),
        P(("blk", "group")),
        P(),
        P(),
    )
    return jax.shard_map(
        per_device,
        mesh=mesh,
        in_specs=placed,
        out_specs=(P(("blk", "group"), None), P(("blk", "group"), None)),
        check_vma=False,
    )
```

```python
import jax
import jax.numpy as jnp
from jax import lax
from jax.experimental import pallas as pl
from jax.experimental.pallas import tpu as pltpu
from jax.sharding import PartitionSpec as P

MESH = pl.DeviceIdType.MESH
F32 = jnp.float32
BF16 = jnp.bfloat16

NY, NX, NZ = 4, 4, 8
SHARD = 8
WIDTH = 1152
ROWS = 512
A0, A1 = 0, 512
B0, B1 = 512, 1024
C0, C1 = 1024, 1152
WIDE = 1280
SPAN = NX * NZ * SHARD
PLANE = NY * SPAN


def place():
    blk = lax.axis_index("blk")
    group = lax.axis_index("group")
    x = (group // 16) * 2 + blk // 4
    return blk % 4, x, (group // 2) % NZ, group % 2


def device(y, x, z, core):
    return ((x % 2) * 4 + y, ((x // 2) * NZ + z) * 2 + core)


def remote(src, dst, sems, index, target):
    return pltpu.make_async_remote_copy(
        src_ref=src,
        dst_ref=dst,
        send_sem=sems[0].at[index],
        recv_sem=sems[1].at[index],
        device_id=target,
        device_id_type=MESH,
    )


def kernel(
    trace_ref, code_ref, tid_ref, cid_ref, scale_ref, shift_ref,
    trace_out, code_out,
    traces, tids, codes, flat, slopes, parts,
    recv_a1, recv_b1, recv_c1, sum_a, sum_b, sum_c, recv_a2, recv_b2, recv_c2,
    sum_ab, sum_c2, recv_ab3, recv_c3, tg_own, tg_send, tg_recv,
    local, s_d, r_d, s_ag, r_ag, s_g3a, r_g3a, s_g3b, r_g3b, s_g3c, r_g3c, s_rs, r_rs,
):
    y, x, z, core = place()
    ag = (s_ag, r_ag)
    rs = (s_rs, r_rs)
    dd = (s_d, r_d)
    g3a, g3b, g3c = (s_g3a, r_g3a), (s_g3b, r_g3b), (s_g3c, r_g3c)

    def on_y(k):
        return device((y + k) % NY, x, z, core)

    def on_x(k):
        return device(y, (x + k) % NX, z, core)

    def on_z(k):
        return device(y, x, (z + k) % NZ, core)

    other = device(y, x, z, 1 - core)

    barrier = pltpu.get_barrier_semaphore()
    partners = [on_y(k) for k in (1, 2, 3)] + [on_x(k) for k in (1, 2, 3)]
    partners += [on_z(k) for k in range(1, NZ)] + [other]
    for partner in partners:
        pl.semaphore_signal(barrier, inc=1, device_id=partner, device_id_type=MESH)

    spread = jnp.broadcast_to(cid_ref[...], (SHARD, SHARD))
    row = lax.broadcasted_iota(jnp.int32, (SHARD, SHARD), 0)
    column = lax.broadcasted_iota(jnp.int32, (SHARD, SHARD), 1)
    ids = jnp.sum(jnp.where(row == column, spread, 0), axis=1, keepdims=True)
    high = (ids // 16).astype(F32)
    low = (ids % 16).astype(F32)
    lane = lax.broadcasted_iota(jnp.int32, (SHARD, 128), 1)
    tile = jnp.where(lane == 0, high, jnp.where(lane == 1, low, 0.0)).astype(BF16)
    codes[y, x, z, :, 0:WIDTH] = code_ref[...]
    codes[y, x, z, :, WIDTH:WIDE] = tile
    pl.semaphore_wait(barrier, len(partners))

    near_z = (1, 7, 2, 6, 3, 5, 4)
    near = (1, 3, 2)
    sent = []

    def go(copy):
        copy.start()
        sent.append(copy)
        return copy

    ref = codes.at[y, x, z, :, A0:B1]
    g1 = [go(remote(ref, ref, ag, k - 1, on_z(k))) for k in near_z]
    ref = codes.at[y, x, z, :, C0:WIDE]
    g1c = [go(remote(ref, ref, ag, 6 + k, on_x(k))) for k in near]

    d0 = pltpu.make_async_copy(trace_ref, traces.at[0:ROWS], local)
    d0.start()
    d1 = remote(trace_ref, traces.at[ROWS : 2 * ROWS], dd, 0, other)
    d2 = remote(tid_ref, tids.at[1], dd, 1, other)
    d1.start()
    d2.start()
    tids[0] = tid_ref[...]

    def gather_a(i, k):
        ref = codes.at[y, (x - i) % NX, :, :, A0:A1]
        return remote(ref, ref, g3a, i * 3 + k - 1, on_y(k))

    def gather_b(j, k):
        ref = codes.at[(y - j) % NY, x, :, :, B0:B1]
        return remote(ref, ref, g3b, j * 3 + k - 1, on_x(k))

    def gather_c(j, k):
        ref = codes.at[(y - j) % NY, :, z, :, C0:WIDE]
        return remote(ref, ref, g3c, j * 7 + k - 1, on_z(k))

    for copy in g1c:
        copy.wait_recv()
    ref = codes.at[y, :, z, :, C0:WIDE]
    g2c = [go(remote(ref, ref, ag, 9 + k, on_y(k))) for k in near]
    for k in near_z:
        go(gather_c(0, k))
    for copy in g1:
        copy.wait_recv()
    ref_a = codes.at[y, x, :, :, A0:A1]
    ref_b = codes.at[y, x, :, :, B0:B1]
    g2a = [go(remote(ref_a, ref_a, ag, 12 + k, on_x(k))) for k in near]
    g2b = [go(remote(ref_b, ref_b, ag, 15 + k, on_y(k))) for k in near]
    for k in near:
        go(gather_a(0, k))
        go(gather_b(0, k))
    for n, i in enumerate(near):
        g2c[n].wait_recv()
        for k in near_z:
            go(gather_c(i, k))
    for n, i in enumerate(near):
        g2a[n].wait_recv()
        for k in near:
            go(gather_a(i, k))
        g2b[n].wait_recv()
        for k in near:
            go(gather_b(i, k))
    d0.wait()
    d1.wait()
    d2.wait()

    scale = jnp.exp(scale_ref[...])
    shift = shift_ref[...]
    trace_ids = jnp.concatenate([tids[0], tids[1]], axis=1).astype(F32)

    def send_a1(j, q):
        return remote(
            parts.at[q, :, :, :, A0:A1], recv_a1.at[j - 1], rs, j - 1, on_y(-j)
        )

    def send_b1(j, q, k):
        return remote(
            parts.at[q, (x + k) % NX, :, :, B0:B1], recv_b1.at[k - 1, q], rs, 3 + j * 3 + k - 1, on_x(k)
        )

    @pl.loop(0, NY)
    def _(step):
        j = step + (step // 2) * (5 - 2 * step)
        q = (y - j) % NY

        @pl.when(j != 0)
        def _():
            for i in range(NX):
                gather_a(i, j).wait_recv()

        for k in range(1, NX):
            gather_b(j, k).wait_recv()
        for k in range(1, NZ):
            gather_c(j, k).wait_recv()
        at = pl.multiple_of(q * SPAN, SPAN)
        for i in range(NX):
            block = codes[q, i, :, :, 0:WIDTH].astype(F32).reshape(NZ * SHARD, WIDTH)
            flat[pl.ds(at + i * NZ * SHARD, NZ * SHARD), :] = block.astype(BF16)
        marks = codes[q, :, :, :, WIDTH:WIDE].astype(F32).reshape(SPAN, 128)
        code_ids = marks[:, 0:1] * 16.0 + marks[:, 1:2]
        logits = lax.dot_general(
            flat[pl.ds(at, SPAN), :], traces[...], (((1,), (1,)), ((), ())), preferred_element_type=F32
        )
        logits = logits * scale + shift
        same = code_ids == trace_ids
        raised = jnp.exp(jnp.where(same, logits, -logits))
        slope = jnp.where(same, -scale, scale) / (1.0 + raised)
        slopes[pl.ds(at, SPAN), :] = slope.astype(BF16)
        grad = jnp.dot(slopes[pl.ds(at, SPAN), :], traces[...], preferred_element_type=F32)
        parts[q] = grad.reshape(NX, NZ, SHARD, WIDTH).astype(BF16)

        @pl.when(j != 0)
        def _():
            send_a1(j, q).start()

        for k in range(1, NX):
            send_b1(j, q, k).start()

    c1 = []
    for k in range(1, NZ):
        c1.append(
            remote(parts.at[:, :, (z + k) % NZ, :, C0:C1], recv_c1.at[k - 1], rs, 14 + k, on_z(k))
        )
        c1[-1].start()

    def trace_rows(first):
        return lax.dot_general(
            slopes[:, first : first + 256], flat[...], (((0,), (0,)), ((), ())), preferred_element_type=F32
        )

    for n in range(2):
        tg_send[n * 256 : n * 256 + 256, :] = trace_rows(ROWS + n * 256)
    d3 = remote(tg_send, tg_recv, dd, 2, other)
    d3.start()
    for n in range(2):
        tg_own[n * 256 : n * 256 + 256, :] = trace_rows(n * 256)

    for copy in c1:
        copy.wait_recv()
    for i in range(NY):
        total = parts[i, :, z, :, C0:C1].astype(F32)
        for k in range(NZ - 1):
            total = total + recv_c1[k, i].astype(F32)
        sum_c[i] = total.astype(BF16)
    c2 = []
    for k in range(1, NY):
        c2.append(remote(sum_c.at[(y + k) % NY], recv_c2.at[k - 1], rs, 21 + k, on_y(k)))
        c2[-1].start()

    for k in range(1, NX):
        for j in range(NY):
            send_b1(j, (y - j) % NY, k).wait_recv()
    for i in range(NY):
        total = parts[i, x, :, :, B0:B1].astype(F32)
        for k in range(NX - 1):
            total = total + recv_b1[k, i].astype(F32)
        sum_b[i] = total.astype(BF16)
    b2 = []
    for k in range(1, NY):
        b2.append(remote(sum_b.at[(y + k) % NY], recv_b2.at[k - 1], rs, 24 + k, on_y(k)))
        b2[-1].start()

    for j in range(1, NY):
        send_a1(j, (y - j) % NY).wait_recv()
    for i in range(NX):
        total = parts[y, i, :, :, A0:A1].astype(F32)
        for k in range(NY - 1):
            total = total + recv_a1[k, i].astype(F32)
        sum_a[i] = total.astype(BF16)
    a2 = []
    for k in range(1, NX):
        a2.append(remote(sum_a.at[(x + k) % NX], recv_a2.at[k - 1], rs, 27 + k, on_x(k)))
        a2[-1].start()

    for copy in c2:
        copy.wait_recv()
    total = sum_c[y].astype(F32)
    for k in range(NY - 1):
        total = total + recv_c2[k].astype(F32)
    sum_c2[...] = total.astype(BF16)
    c3 = []
    for k in range(1, NX):
        c3.append(remote(sum_c2.at[(x + k) % NX], recv_c3.at[k - 1], rs, 30 + k, on_x(k)))
        c3[-1].start()
    for copy in b2:
        copy.wait_recv()
    total = sum_b[y].astype(F32)
    for k in range(NY - 1):
        total = total + recv_b2[k].astype(F32)
    sum_ab[:, :, B0:B1] = total.astype(BF16)
    for copy in a2:
        copy.wait_recv()
    total = sum_a[x].astype(F32)
    for k in range(NX - 1):
        total = total + recv_a2[k].astype(F32)
    sum_ab[:, :, A0:A1] = total.astype(BF16)
    ab3 = []
    for k in range(1, NZ):
        ab3.append(remote(sum_ab.at[(z + k) % NZ], recv_ab3.at[k - 1], rs, 33 + k, on_z(k)))
        ab3[-1].start()

    d3.wait()
    trace_out[...] = (tg_own[...] + tg_recv[...]).astype(BF16)

    for copy in c3:
        copy.wait_recv()
    total = sum_c2[x].astype(F32)
    for k in range(NX - 1):
        total = total + recv_c3[k].astype(F32)
    code_out[:, C0:C1] = total.astype(BF16)
    for copy in ab3:
        copy.wait_recv()
    total = sum_ab[z].astype(F32)
    for k in range(NZ - 1):
        total = total + recv_ab3[k].astype(F32)
    code_out[:, A0:B1] = total.astype(BF16)

    for copy in sent + c1 + c2 + b2 + a2 + c3 + ab3:
        copy.wait_send()
    for j in range(NY):
        if j:
            send_a1(j, (y - j) % NY).wait_send()
        for k in range(1, NX):
            send_b1(j, (y - j) % NY, k).wait_send()


def per_device(trace_emb, code_emb, trace_ids, code_ids, log_scale, bias):
    vmem = pl.BlockSpec(memory_space=pltpu.VMEM)
    dma = pltpu.SemaphoreType.DMA
    scratch = [
        pltpu.VMEM((2 * ROWS, WIDTH), BF16),
        pltpu.VMEM((2, 1, ROWS), jnp.int32),
        pltpu.VMEM((NY, NX, NZ, SHARD, WIDE), BF16),
        pltpu.VMEM((PLANE, WIDTH), BF16),
        pltpu.VMEM((PLANE, 2 * ROWS), BF16),
        pltpu.VMEM((NY, NX, NZ, SHARD, WIDTH), BF16),
        pltpu.VMEM((NY - 1, NX, NZ, SHARD, A1 - A0), BF16),
        pltpu.VMEM((NX - 1, NY, NZ, SHARD, B1 - B0), BF16),
        pltpu.VMEM((NZ - 1, NY, NX, SHARD, C1 - C0), BF16),
        pltpu.VMEM((NX, NZ, SHARD, A1 - A0), BF16),
        pltpu.VMEM((NY, NZ, SHARD, B1 - B0), BF16),
        pltpu.VMEM((NY, NX, SHARD, C1 - C0), BF16),
        pltpu.VMEM((NX - 1, NZ, SHARD, A1 - A0), BF16),
        pltpu.VMEM((NY - 1, NZ, SHARD, B1 - B0), BF16),
        pltpu.VMEM((NY - 1, NX, SHARD, C1 - C0), BF16),
        pltpu.VMEM((NZ, SHARD, B1 - A0), BF16),
        pltpu.VMEM((NX, SHARD, C1 - C0), BF16),
        pltpu.VMEM((NZ - 1, SHARD, B1 - A0), BF16),
        pltpu.VMEM((NX - 1, SHARD, C1 - C0), BF16),
        pltpu.VMEM((ROWS, WIDTH), F32),
        pltpu.VMEM((ROWS, WIDTH), F32),
        pltpu.VMEM((ROWS, WIDTH), F32),
        dma,
        dma((3,)),
        dma((3,)),
        dma((19,)),
        dma((19,)),
        dma((12,)),
        dma((12,)),
        dma((12,)),
        dma((12,)),
        dma((28,)),
        dma((28,)),
        dma((41,)),
        dma((41,)),
    ]
    return pl.pallas_call(
        kernel,
        out_shape=(pltpu.VMEM((ROWS, WIDTH), BF16), pltpu.VMEM((SHARD, WIDTH), BF16)),
        in_specs=[pl.BlockSpec(memory_space=pl.ANY)] + [vmem] * 5,
        out_specs=(vmem, vmem),
        scratch_shapes=scratch,
        compiler_params=pltpu.CompilerParams(
            collective_id=0, has_side_effects=True, vmem_limit_bytes=56 * 2**20
        ),
        name="contrast",
    )(
        trace_emb,
        code_emb,
        trace_ids.reshape(1, ROWS),
        code_ids.reshape(1, SHARD),
        log_scale.reshape(1, 1),
        bias.reshape(1, 1),
    )


def solution(mesh):
    placed = (
        P(("blk", "group"), None),
        P(("blk", "group"), None),
        P(("blk", "group")),
        P(("blk", "group")),
        P(),
        P(),
    )
    return jax.shard_map(
        per_device,
        mesh=mesh,
        in_specs=placed,
        out_specs=(P(("blk", "group"), None), P(("blk", "group"), None)),
        check_vma=False,
    )
```

```python
import jax
import jax.numpy as jnp
from jax import lax
from jax.experimental import pallas as pl
from jax.experimental.pallas import tpu as pltpu
from jax.sharding import PartitionSpec as P

MESH = pl.DeviceIdType.MESH
F32 = jnp.float32
BF16 = jnp.bfloat16

NY, NX, NZ = 4, 4, 8
SHARD = 8
WIDTH = 1152
ROWS = 512
A0, A1 = 0, 384
B0, B1 = 384, 768
C0, C1 = 768, 1152
GA = slice(0, 384)
GB = slice(384, 768)
GAB = slice(0, 768)
GM = slice(768, 896)
GABM = slice(0, 896)
GC = slice(896, 1280)
WIDE = 1280
SPAN = NX * NZ * SHARD
PLANE = NY * SPAN


def place():
    blk = lax.axis_index("blk")
    group = lax.axis_index("group")
    x = (group // 16) * 2 + blk // 4
    return blk % 4, x, (group // 2) % NZ, group % 2


def device(y, x, z, core):
    return ((x % 2) * 4 + y, ((x // 2) * NZ + z) * 2 + core)


def remote(src, dst, sems, index, target):
    return pltpu.make_async_remote_copy(
        src_ref=src,
        dst_ref=dst,
        send_sem=sems[0].at[index],
        recv_sem=sems[1].at[index],
        device_id=target,
        device_id_type=MESH,
    )


def kernel(
    trace_ref, code_ref, tid_ref, cid_ref, scale_ref, shift_ref,
    trace_out, code_out,
    traces, tids, codes, marks, flat, slopes, parts,
    recv_a1, recv_b1, recv_c1, sum_z, sum_a, sum_b, sum_c, recv_a2, recv_b2, recv_c2,
    sum_ab, recv_ab3, tg_own, tg_send, tg_recv,
    local, s_d, r_d, s_ag, r_ag, s_g3a, r_g3a, s_g3b, r_g3b, s_g3c, r_g3c, s_g1p, r_g1p, s_rs, r_rs, s_rsc, r_rsc, s_rsp, r_rsp,
):
    y, x, z, core = place()
    ag = (s_ag, r_ag)
    rs = (s_rs, r_rs)
    dd = (s_d, r_d)
    g3a, g3b, g3c = (s_g3a, r_g3a), (s_g3b, r_g3b), (s_g3c, r_g3c)
    g1p, rsc, rsp = (s_g1p, r_g1p), (s_rsc, r_rsc), (s_rsp, r_rsp)

    def on_y(k):
        return device((y + k) % NY, x, z, core)

    def on_x(k):
        return device(y, (x + k) % NX, z, core)

    def on_z(k):
        return device(y, x, (z + k) % NZ, core)

    def on_plane(j, i):
        return device((y + j) % NY, (x + i) % NX, z, core)

    other = device(y, x, z, 1 - core)

    barrier = pltpu.get_barrier_semaphore()
    in_plane = [(j, i) for j in (0, 1, 3, 2) for i in (0, 1, 3, 2) if (j, i) != (0, 0)]
    partners = [on_plane(j, i) for j, i in in_plane]
    partners += [on_z(k) for k in range(1, NZ)] + [other]
    for partner in partners:
        pl.semaphore_signal(barrier, inc=1, device_id=partner, device_id_type=MESH)

    spread = jnp.broadcast_to(cid_ref[...], (SHARD, SHARD))
    row = lax.broadcasted_iota(jnp.int32, (SHARD, SHARD), 0)
    column = lax.broadcasted_iota(jnp.int32, (SHARD, SHARD), 1)
    ids = jnp.sum(jnp.where(row == column, spread, 0), axis=1, keepdims=True)
    high = (ids // 16).astype(F32)
    low = (ids % 16).astype(F32)
    lane = lax.broadcasted_iota(jnp.int32, (SHARD, 128), 1)
    tile = jnp.where(lane == 2 * z, high, jnp.where(lane == 2 * z + 1, low, 0.0)).astype(BF16)
    codes[y, x, z, :, GAB] = code_ref[:, 0:768]
    codes[y, x, z, :, GM] = tile
    codes[y, x, z, :, GC] = code_ref[:, 768:WIDTH]
    pl.semaphore_wait(barrier, len(partners))

    near_z = (1, 7, 2, 6, 3, 5, 4)
    near = (1, 3, 2)
    sent = []

    def go(copy):
        copy.start()
        sent.append(copy)
        return copy

    ref = codes.at[y, x, z, :, GABM]
    g1 = [go(remote(ref, ref, ag, k - 1, on_z(k))) for k in near_z]
    ref = codes.at[y, x, z, :, GC]
    g1c = {(j, i): go(remote(ref, ref, g1p, j * 4 + i, on_plane(j, i))) for j, i in in_plane}

    d0 = pltpu.make_async_copy(trace_ref, traces.at[0:ROWS], local)
    d0.start()
    d1 = remote(trace_ref, traces.at[ROWS : 2 * ROWS], dd, 0, other)
    d2 = remote(tid_ref, tids.at[1], dd, 1, other)
    d1.start()
    d2.start()
    tids[0] = tid_ref[...]

    def gather_a(i, way, hop):
        step = 1 - 2 * way
        ref = codes.at[(y - step * (hop - 1)) % NY, (x - i) % NX, :, :, GA]
        return remote(ref, ref, g3a, (way * 4 + i) * 2 + hop - 1, on_y(step))

    def gather_b(j, way, hop):
        step = 1 - 2 * way
        ref = codes.at[(y - j) % NY, (x - step * (hop - 1)) % NX, :, :, GB]
        return remote(ref, ref, g3b, (way * 4 + j) * 2 + hop - 1, on_x(step))

    def gather_c(j, kind):
        half = 2 - 4 * (j // 2)
        start, step = ((0, 1), (0, -1), (0, 2), (0, -2), (-2, 1), (2, -1), (-half, half))[kind]
        ref = codes.at[(y - j) % NY, :, (z + start) % NZ, :, GC]
        return remote(ref, ref, g3c, j * 7 + kind, on_z(step))

    def pass_on(gather, n, way):
        gather(n, way, 1).wait_recv()
        go(gather(n, way, 2))

    def set_out(gather, n):
        for way in (0, 1):
            go(gather(n, way, 1))

    def set_out_c(j):
        for i in near if j == 0 else (0, 1, 3, 2):
            g1c[j, i].wait_recv()
        for kind in (2, 3, 0, 1):
            go(gather_c(j, kind))

    def pass_on_c(j):
        gather_c(j, 2).wait_recv()
        go(gather_c(j, 4))
        if j < 2:
            go(gather_c(j, 6))
        gather_c(j, 3).wait_recv()
        go(gather_c(j, 5))
        if j >= 2:
            go(gather_c(j, 6))

    for j in (0, 1, 3, 2):
        set_out_c(j)
    for copy in g1:
        copy.wait_recv()
    ref_a = codes.at[y, x, :, :, GA]
    ref_b = codes.at[y, x, :, :, GB]
    g2a = [go(remote(ref_a, ref_a, ag, 12 + k, on_x(k))) for k in near]
    g2b = [go(remote(ref_b, ref_b, ag, 15 + k, on_y(k))) for k in near]
    set_out(gather_a, 0)
    set_out(gather_b, 0)
    marks[y, x] = jnp.sum(codes[y, x, :, :, GM].astype(F32), axis=0).astype(BF16)
    ref = marks.at[y, x]
    m2 = [go(remote(ref, ref, ag, 18 + k, on_x(k))) for k in near]
    pass_on_c(0)
    for n in (0, 1):
        g2a[n].wait_recv()
        set_out(gather_a, near[n])
        g2b[n].wait_recv()
        set_out(gather_b, near[n])
    pass_on(gather_a, 0, 0)
    pass_on(gather_b, 0, 0)
    g2a[2].wait_recv()
    set_out(gather_a, 2)
    g2b[2].wait_recv()
    set_out(gather_b, 2)
    pass_on_c(1)
    for copy in m2:
        copy.wait_recv()
    ref = marks.at[y]
    m3 = [go(remote(ref, ref, ag, 21 + k, on_y(k))) for k in near]
    pass_on_c(3)
    pass_on(gather_a, 3, 1)
    pass_on(gather_b, 3, 1)
    pass_on(gather_a, 1, 0)
    pass_on(gather_b, 1, 0)
    pass_on_c(2)
    pass_on(gather_a, 2, 1)
    pass_on(gather_b, 2, 1)
    for copy in m3:
        copy.wait_recv()
    d0.wait()
    d1.wait()
    d2.wait()

    scale = jnp.exp(scale_ref[...])
    shift = shift_ref[...]
    trace_ids = jnp.concatenate([tids[0], tids[1]], axis=1).astype(F32)

    lane = lax.broadcasted_iota(jnp.int32, (1, NZ, 1, 128), 3)
    owner = lax.broadcasted_iota(jnp.int32, (1, NZ, 1, 128), 1)
    pick = jnp.where(lane == 2 * owner, 16.0, jnp.where(lane == 2 * owner + 1, 1.0, 0.0))

    def send_a1(j, q):
        return remote(
            parts.at[q, :, :, :, A0:A1], recv_a1.at[j - 1], rs, j - 1, on_y(-j)
        )

    def send_b1(j, q, k):
        return remote(
            parts.at[q, (x + k) % NX, :, :, B0:B1], recv_b1.at[k - 1, q], rs, 3 + j * 3 + k - 1, on_x(k)
        )

    def send_c1(j, kind):
        q = (y - j) % NY
        half = 2 - 4 * (j // 2)
        if kind in (2, 3):
            source = sum_z.at[kind - 2, q]
        else:
            away = (1, -1, None, None, 3, -3, 4)[kind]
            source = parts.at[q, :, (z + away) % NZ, :, C0:C1]
        step = (1, -1, 2, -2, 1, -1, half)[kind]
        return remote(source, recv_c1.at[kind, q], rsc, j * 7 + kind, on_z(step))

    def relay_c(j):
        q = (y - j) % NY
        for kind in (4, 5, 6):
            send_c1(j, kind).wait_recv()
        upper = jnp.where(j < 2, 1.0, 0.0)
        middle = recv_c1[6, q].astype(F32)
        total = parts[q, :, (z + 2) % NZ, :, C0:C1].astype(F32) + recv_c1[4, q].astype(F32) + upper * middle
        sum_z[0, q] = total.astype(BF16)
        total = parts[q, :, (z + 6) % NZ, :, C0:C1].astype(F32) + recv_c1[5, q].astype(F32) + (1.0 - upper) * middle
        sum_z[1, q] = total.astype(BF16)
        send_c1(j, 2).start()
        send_c1(j, 3).start()

    def block_at(step):
        return step + (step // 2) * (5 - 2 * step)

    @pl.loop(0, NY)
    def _(step):
        j = block_at(step)
        q = (y - j) % NY

        @pl.when(j == 1)
        def _():
            gather_a(2, 0, 1).wait_recv()
            gather_a(3, 0, 1).wait_recv()

        @pl.when(j == 3)
        def _():
            gather_a(0, 1, 1).wait_recv()
            gather_a(1, 1, 1).wait_recv()

        @pl.when(j == 2)
        def _():
            for i in range(NX):
                gather_a(i, i // 2, 2).wait_recv()

        gather_b(j, 1 - j // 2, 1).wait_recv()
        gather_b(j, j // 2, 2).wait_recv()
        for kind in (0, 1, 4, 5, 6):
            gather_c(j, kind).wait_recv()
        at = pl.multiple_of(q * SPAN, SPAN)
        for i in range(NX):
            rows = pl.ds(at + i * NZ * SHARD, NZ * SHARD)
            block = codes[q, i, :, :, GAB].astype(F32).reshape(NZ * SHARD, 768)
            flat[rows, 0:768] = block.astype(BF16)
            block = codes[q, i, :, :, GC].astype(F32).reshape(NZ * SHARD, 384)
            flat[rows, 768:WIDTH] = block.astype(BF16)
        spread = marks[q].astype(F32).reshape(NX, 1, SHARD, 128)
        code_ids = jnp.sum(spread * pick, axis=3, keepdims=True).reshape(SPAN, 1)
        logits = lax.dot_general(
            flat[pl.ds(at, SPAN), :], traces[...], (((1,), (1,)), ((), ())), preferred_element_type=F32
        )
        logits = logits * scale + shift
        same = code_ids == trace_ids
        raised = jnp.exp(jnp.where(same, logits, -logits))
        slope = jnp.where(same, -scale, scale) / (1.0 + raised)
        slopes[pl.ds(at, SPAN), :] = slope.astype(BF16)
        grad = jnp.dot(slopes[pl.ds(at, SPAN), :], traces[...], preferred_element_type=F32)
        parts[q] = grad.reshape(NX, NZ, SHARD, WIDTH).astype(BF16)

        @pl.when(j != 0)
        def _():
            send_a1(j, q).start()

        for kind in (4, 5, 6):
            send_c1(j, kind).start()
        for k in range(1, NX):
            send_b1(j, q, k).start()
        for kind in (0, 1):
            send_c1(j, kind).start()

        @pl.when(step >= 2)
        def _():
            relay_c(block_at(step - 2))

    relay_c(3)

    def trace_rows(first):
        return lax.dot_general(
            slopes[:, first : first + 256], flat[...], (((0,), (0,)), ((), ())), preferred_element_type=F32
        )

    for n in range(2):
        tg_send[n * 256 : n * 256 + 256, :] = trace_rows(ROWS + n * 256)
    d3 = remote(tg_send, tg_recv, dd, 2, other)
    d3.start()
    relay_c(2)
    for n in range(2):
        tg_own[n * 256 : n * 256 + 256, :] = trace_rows(n * 256)

    for k in range(1, NX):
        for j in range(NY):
            send_b1(j, (y - j) % NY, k).wait_recv()
    for i in range(NY):
        total = parts[i, x, :, :, B0:B1].astype(F32)
        for k in range(NX - 1):
            total = total + recv_b1[k, i].astype(F32)
        sum_b[i] = total.astype(BF16)
    b2 = []
    for k in range(1, NY):
        b2.append(remote(sum_b.at[(y + k) % NY], recv_b2.at[k - 1], rs, 24 + k, on_y(k)))
        b2[-1].start()

    for j in range(1, NY):
        send_a1(j, (y - j) % NY).wait_recv()
    for i in range(NX):
        total = parts[y, i, :, :, A0:A1].astype(F32)
        for k in range(NY - 1):
            total = total + recv_a1[k, i].astype(F32)
        sum_a[i] = total.astype(BF16)
    a2 = []
    for k in range(1, NX):
        a2.append(remote(sum_a.at[(x + k) % NX], recv_a2.at[k - 1], rs, 27 + k, on_x(k)))
        a2[-1].start()

    for j in range(NY):
        for kind in range(4):
            send_c1(j, kind).wait_recv()
    for i in range(NY):
        total = parts[i, :, z, :, C0:C1].astype(F32)
        for kind in range(4):
            total = total + recv_c1[kind, i].astype(F32)
        sum_c[i] = total.astype(BF16)
    c2 = []
    for j, i in in_plane:
        c2.append(
            remote(sum_c.at[(y + j) % NY, (x + i) % NX], recv_c2.at[j * 4 + i], rsp, j * 4 + i, on_plane(j, i))
        )
        c2[-1].start()
    for copy in b2:
        copy.wait_recv()
    total = sum_b[y].astype(F32)
    for k in range(NY - 1):
        total = total + recv_b2[k].astype(F32)
    sum_ab[:, :, B0:B1] = total.astype(BF16)
    for copy in a2:
        copy.wait_recv()
    total = sum_a[x].astype(F32)
    for k in range(NX - 1):
        total = total + recv_a2[k].astype(F32)
    sum_ab[:, :, A0:A1] = total.astype(BF16)
    ab3 = []
    for k in range(1, NZ):
        ab3.append(remote(sum_ab.at[(z + k) % NZ], recv_ab3.at[k - 1], rs, 33 + k, on_z(k)))
        ab3[-1].start()

    d3.wait()
    trace_out[...] = (tg_own[...] + tg_recv[...]).astype(BF16)

    for copy in c2:
        copy.wait_recv()
    total = sum_c[y, x].astype(F32)
    for j, i in in_plane:
        total = total + recv_c2[j * 4 + i].astype(F32)
    code_out[:, C0:C1] = total.astype(BF16)
    for copy in ab3:
        copy.wait_recv()
    total = sum_ab[z].astype(F32)
    for k in range(NZ - 1):
        total = total + recv_ab3[k].astype(F32)
    code_out[:, A0:B1] = total.astype(BF16)

    for copy in sent + c2 + b2 + a2 + ab3:
        copy.wait_send()
    for j in range(NY):
        if j:
            send_a1(j, (y - j) % NY).wait_send()
        for k in range(1, NX):
            send_b1(j, (y - j) % NY, k).wait_send()
        for kind in range(7):
            send_c1(j, kind).wait_send()


def per_device(trace_emb, code_emb, trace_ids, code_ids, log_scale, bias):
    vmem = pl.BlockSpec(memory_space=pltpu.VMEM)
    dma = pltpu.SemaphoreType.DMA
    scratch = [
        pltpu.VMEM((2 * ROWS, WIDTH), BF16),
        pltpu.VMEM((2, 1, ROWS), jnp.int32),
        pltpu.VMEM((NY, NX, NZ, SHARD, WIDE), BF16),
        pltpu.VMEM((NY, NX, SHARD, 128), BF16),
        pltpu.VMEM((PLANE, WIDTH), BF16),
        pltpu.VMEM((PLANE, 2 * ROWS), BF16),
        pltpu.VMEM((NY, NX, NZ, SHARD, WIDTH), BF16),
        pltpu.VMEM((NY - 1, NX, NZ, SHARD, A1 - A0), BF16),
        pltpu.VMEM((NX - 1, NY, NZ, SHARD, B1 - B0), BF16),
        pltpu.VMEM((7, NY, NX, SHARD, C1 - C0), BF16),
        pltpu.VMEM((2, NY, NX, SHARD, C1 - C0), BF16),
        pltpu.VMEM((NX, NZ, SHARD, A1 - A0), BF16),
        pltpu.VMEM((NY, NZ, SHARD, B1 - B0), BF16),
        pltpu.VMEM((NY, NX, SHARD, C1 - C0), BF16),
        pltpu.VMEM((NX - 1, NZ, SHARD, A1 - A0), BF16),
        pltpu.VMEM((NY - 1, NZ, SHARD, B1 - B0), BF16),
        pltpu.VMEM((NY * NX, SHARD, C1 - C0), BF16),
        pltpu.VMEM((NZ, SHARD, B1 - A0), BF16),
        pltpu.VMEM((NZ - 1, SHARD, B1 - A0), BF16),
        pltpu.VMEM((ROWS, WIDTH), F32),
        pltpu.VMEM((ROWS, WIDTH), F32),
        pltpu.VMEM((ROWS, WIDTH), F32),
        dma,
        dma((3,)),
        dma((3,)),
        dma((25,)),
        dma((25,)),
        dma((16,)),
        dma((16,)),
        dma((16,)),
        dma((16,)),
        dma((28,)),
        dma((28,)),
        dma((16,)),
        dma((16,)),
        dma((41,)),
        dma((41,)),
        dma((28,)),
        dma((28,)),
        dma((16,)),
        dma((16,)),
    ]
    return pl.pallas_call(
        kernel,
        out_shape=(pltpu.VMEM((ROWS, WIDTH), BF16), pltpu.VMEM((SHARD, WIDTH), BF16)),
        in_specs=[pl.BlockSpec(memory_space=pl.ANY)] + [vmem] * 5,
        out_specs=(vmem, vmem),
        scratch_shapes=scratch,
        compiler_params=pltpu.CompilerParams(
            collective_id=0, has_side_effects=True, vmem_limit_bytes=56 * 2**20
        ),
        name="contrast",
    )(
        trace_emb,
        code_emb,
        trace_ids.reshape(1, ROWS),
        code_ids.reshape(1, SHARD),
        log_scale.reshape(1, 1),
        bias.reshape(1, 1),
    )


def solution(mesh):
    placed = (
        P(("blk", "group"), None),
        P(("blk", "group"), None),
        P(("blk", "group")),
        P(("blk", "group")),
        P(),
        P(),
    )
    return jax.shard_map(
        per_device,
        mesh=mesh,
        in_specs=placed,
        out_specs=(P(("blk", "group"), None), P(("blk", "group"), None)),
        check_vma=False,
    )
```

```python
import jax
import jax.numpy as jnp
from jax import lax
from jax.experimental import pallas as pl
from jax.experimental.pallas import tpu as pltpu
from jax.sharding import PartitionSpec as P

MESH = pl.DeviceIdType.MESH
F32 = jnp.float32
BF16 = jnp.bfloat16

NY, NX, NZ = 4, 4, 8
SHARD = 8
WIDTH = 1152
ROWS = 512
A0, A1 = 0, 384
B0, B1 = 384, 768
C0, C1 = 768, 1152
GA = slice(0, 384)
GB = slice(384, 768)
GAB = slice(0, 768)
GM = slice(768, 896)
GABM = slice(0, 896)
GC = slice(896, 1280)
WIDE = 1280
SPAN = NX * NZ * SHARD
PLANE = NY * SPAN


def place():
    blk = lax.axis_index("blk")
    group = lax.axis_index("group")
    x = (group // 16) * 2 + blk // 4
    return blk % 4, x, (group // 2) % NZ, group % 2


def device(y, x, z, core):
    return ((x % 2) * 4 + y, ((x // 2) * NZ + z) * 2 + core)


def remote(src, dst, sems, index, target):
    return pltpu.make_async_remote_copy(
        src_ref=src,
        dst_ref=dst,
        send_sem=sems[0].at[index],
        recv_sem=sems[1].at[index],
        device_id=target,
        device_id_type=MESH,
    )


def kernel(
    trace_ref, code_ref, tid_ref, cid_ref, scale_ref, shift_ref,
    trace_out, code_out,
    code_v, cid_v, scale_v, shift_v, traces, tids, codes, marks, flat, slopes, parts,
    recv_a1, recv_b1, recv_c1, sum_z, sum_a, sum_b, sum_c, recv_a2, recv_b2, recv_c2,
    sum_ab, recv_ab3, tg_own, tg_send, tg_recv,
    local, s_d, r_d, s_ag, r_ag, s_g3a, r_g3a, s_g3b, r_g3b, s_g3c, r_g3c, s_g1p, r_g1p, s_rs, r_rs, s_rsc, r_rsc, s_rsp, r_rsp,
):
    y, x, z, core = place()
    ag = (s_ag, r_ag)
    rs = (s_rs, r_rs)
    dd = (s_d, r_d)
    g3a, g3b, g3c = (s_g3a, r_g3a), (s_g3b, r_g3b), (s_g3c, r_g3c)
    g1p, rsc, rsp = (s_g1p, r_g1p), (s_rsc, r_rsc), (s_rsp, r_rsp)

    def on_y(k):
        return device((y + k) % NY, x, z, core)

    def on_x(k):
        return device(y, (x + k) % NX, z, core)

    def on_z(k):
        return device(y, x, (z + k) % NZ, core)

    def on_plane(j, i):
        return device((y + j) % NY, (x + i) % NX, z, core)

    other = device(y, x, z, 1 - core)

    pairs = (
        (trace_ref, traces.at[0:ROWS]), (code_ref, code_v), (cid_ref, cid_v),
        (tid_ref, tids.at[0]), (scale_ref, scale_v), (shift_ref, shift_v),
    )
    fetch = [pltpu.make_async_copy(src, dst, local.at[n]) for n, (src, dst) in enumerate(pairs)]
    for n in (1, 2, 0, 3, 4, 5):
        fetch[n].start()

    barrier = pltpu.get_barrier_semaphore()
    in_plane = [(j, i) for j in (0, 1, 3, 2) for i in (0, 1, 3, 2) if (j, i) != (0, 0)]
    partners = [on_plane(j, i) for j, i in in_plane]
    partners += [on_z(k) for k in range(1, NZ)] + [other]
    for partner in partners:
        pl.semaphore_signal(barrier, inc=1, device_id=partner, device_id_type=MESH)

    fetch[1].wait()
    fetch[2].wait()
    spread = jnp.broadcast_to(cid_v[...], (SHARD, SHARD))
    row = lax.broadcasted_iota(jnp.int32, (SHARD, SHARD), 0)
    column = lax.broadcasted_iota(jnp.int32, (SHARD, SHARD), 1)
    ids = jnp.sum(jnp.where(row == column, spread, 0), axis=1, keepdims=True)
    high = (ids // 16).astype(F32)
    low = (ids % 16).astype(F32)
    lane = lax.broadcasted_iota(jnp.int32, (SHARD, 128), 1)
    tile = jnp.where(lane == 2 * z, high, jnp.where(lane == 2 * z + 1, low, 0.0)).astype(BF16)
    codes[y, x, z, :, GAB] = code_v[:, 0:768]
    codes[y, x, z, :, GM] = tile
    codes[y, x, z, :, GC] = code_v[:, 768:WIDTH]
    pl.semaphore_wait(barrier, len(partners))

    near_z = (1, 7, 2, 6, 3, 5, 4)
    near = (1, 3, 2)
    sent = []

    def go(copy):
        copy.start()
        sent.append(copy)
        return copy

    ref = codes.at[y, x, z, :, GABM]
    g1 = [go(remote(ref, ref, ag, k - 1, on_z(k))) for k in near_z]
    ref = codes.at[y, x, z, :, GC]
    g1c = {(j, i): go(remote(ref, ref, g1p, j * 4 + i, on_plane(j, i))) for j, i in in_plane}

    d1 = remote(trace_ref, traces.at[ROWS : 2 * ROWS], dd, 0, other)
    d2 = remote(tid_ref, tids.at[1], dd, 1, other)
    d1.start()
    d2.start()

    def gather_a(i, way, hop):
        step = 1 - 2 * way
        ref = codes.at[(y - step * (hop - 1)) % NY, (x - i) % NX, :, :, GA]
        return remote(ref, ref, g3a, (way * 4 + i) * 2 + hop - 1, on_y(step))

    def gather_b(j, way, hop):
        step = 1 - 2 * way
        ref = codes.at[(y - j) % NY, (x - step * (hop - 1)) % NX, :, :, GB]
        return remote(ref, ref, g3b, (way * 4 + j) * 2 + hop - 1, on_x(step))

    def gather_c(j, kind):
        half = 2 - 4 * (j // 2)
        start, step = ((0, 1), (0, -1), (0, 2), (0, -2), (-2, 1), (2, -1), (-half, half))[kind]
        ref = codes.at[(y - j) % NY, :, (z + start) % NZ, :, GC]
        return remote(ref, ref, g3c, j * 7 + kind, on_z(step))

    def pass_on(gather, n, way):
        gather(n, way, 1).wait_recv()
        go(gather(n, way, 2))

    def set_out(gather, n):
        for way in (0, 1):
            go(gather(n, way, 1))

    def set_out_c(j):
        for i in near if j == 0 else (0, 1, 3, 2):
            g1c[j, i].wait_recv()
        for kind in (2, 3, 0, 1):
            go(gather_c(j, kind))

    def pass_on_c(j):
        gather_c(j, 2).wait_recv()
        go(gather_c(j, 4))
        if j < 2:
            go(gather_c(j, 6))
        gather_c(j, 3).wait_recv()
        go(gather_c(j, 5))
        if j >= 2:
            go(gather_c(j, 6))

    for j in (0, 1, 3, 2):
        set_out_c(j)
    for copy in g1:
        copy.wait_recv()
    ref_a = codes.at[y, x, :, :, GA]
    ref_b = codes.at[y, x, :, :, GB]
    g2a = [go(remote(ref_a, ref_a, ag, 12 + k, on_x(k))) for k in near]
    g2b = [go(remote(ref_b, ref_b, ag, 15 + k, on_y(k))) for k in near]
    set_out(gather_a, 0)
    set_out(gather_b, 0)
    marks[y, x] = jnp.sum(codes[y, x, :, :, GM].astype(F32), axis=0).astype(BF16)
    ref = marks.at[y, x]
    m2 = [go(remote(ref, ref, ag, 18 + k, on_x(k))) for k in near]
    pass_on_c(0)
    for n in (0, 1):
        g2a[n].wait_recv()
        set_out(gather_a, near[n])
        g2b[n].wait_recv()
        set_out(gather_b, near[n])
    pass_on(gather_a, 0, 0)
    pass_on(gather_b, 0, 0)
    g2a[2].wait_recv()
    set_out(gather_a, 2)
    g2b[2].wait_recv()
    set_out(gather_b, 2)
    pass_on_c(1)
    for copy in m2:
        copy.wait_recv()
    ref = marks.at[y]
    m3 = [go(remote(ref, ref, ag, 21 + k, on_y(k))) for k in near]
    pass_on_c(3)
    pass_on(gather_a, 3, 1)
    pass_on(gather_b, 3, 1)
    pass_on(gather_a, 1, 0)
    pass_on(gather_b, 1, 0)
    pass_on_c(2)
    pass_on(gather_a, 2, 1)
    pass_on(gather_b, 2, 1)
    for copy in m3:
        copy.wait_recv()
    for n in (0, 3, 4, 5):
        fetch[n].wait()
    d1.wait()
    d2.wait()

    scale = jnp.exp(scale_v[...])
    shift = shift_v[...]
    trace_ids = jnp.concatenate([tids[0], tids[1]], axis=1).astype(F32)

    lane = lax.broadcasted_iota(jnp.int32, (1, NZ, 1, 128), 3)
    owner = lax.broadcasted_iota(jnp.int32, (1, NZ, 1, 128), 1)
    pick = jnp.where(lane == 2 * owner, 16.0, jnp.where(lane == 2 * owner + 1, 1.0, 0.0))

    def send_a1(j, i):
        q = (y - j) % NY
        return remote(
            parts.at[q, (x + i) % NX, :, :, A0:A1], recv_a1.at[j - 1, i], rs, (j - 1) * 4 + i, on_y(-j)
        )

    def send_b1(j, k):
        q = (y - j) % NY
        return remote(
            parts.at[q, (x + k) % NX, :, :, B0:B1], recv_b1.at[k - 1, j], rs, 12 + j * 3 + k - 1, on_x(k)
        )

    def send_b2(j):
        return remote(sum_b.at[j], recv_b2.at[j - 1], rs, 23 + j, on_y(-j))

    def relay_b(j):
        for k in near:
            send_b1(j, k).wait_recv()
        total = parts[(y - j) % NY, x, :, :, B0:B1].astype(F32)
        for k in near:
            total = total + recv_b1[k - 1, j].astype(F32)
        sum_b[j] = total.astype(BF16)

    def send_c1(j, kind):
        q = (y - j) % NY
        half = 2 - 4 * (j // 2)
        if kind in (2, 3):
            source = sum_z.at[kind - 2, q]
        else:
            away = (1, -1, None, None, 3, -3, 4)[kind]
            source = parts.at[q, :, (z + away) % NZ, :, C0:C1]
        step = (1, -1, 2, -2, 1, -1, half)[kind]
        return remote(source, recv_c1.at[kind, q], rsc, j * 7 + kind, on_z(step))

    def relay_c(j):
        q = (y - j) % NY
        for kind in (4, 5, 6):
            send_c1(j, kind).wait_recv()
        upper = jnp.where(j < 2, 1.0, 0.0)
        middle = recv_c1[6, q].astype(F32)
        total = parts[q, :, (z + 2) % NZ, :, C0:C1].astype(F32) + recv_c1[4, q].astype(F32) + upper * middle
        sum_z[0, q] = total.astype(BF16)
        total = parts[q, :, (z + 6) % NZ, :, C0:C1].astype(F32) + recv_c1[5, q].astype(F32) + (1.0 - upper) * middle
        sum_z[1, q] = total.astype(BF16)
        send_c1(j, 2).start()
        send_c1(j, 3).start()

    def block_at(step):
        return step + (step // 2) * (5 - 2 * step)

    @pl.loop(0, NY)
    def _(step):
        j = block_at(step)
        q = (y - j) % NY

        @pl.when(j == 1)
        def _():
            gather_a(2, 0, 1).wait_recv()
            gather_a(3, 0, 1).wait_recv()

        @pl.when(j == 3)
        def _():
            gather_a(0, 1, 1).wait_recv()
            gather_a(1, 1, 1).wait_recv()

        @pl.when(j == 2)
        def _():
            for i in range(NX):
                gather_a(i, i // 2, 2).wait_recv()

        gather_b(j, 1 - j // 2, 1).wait_recv()
        gather_b(j, j // 2, 2).wait_recv()
        for kind in (0, 1, 4, 5, 6):
            gather_c(j, kind).wait_recv()
        at = pl.multiple_of(q * SPAN, SPAN)
        for i in range(NX):
            rows = pl.ds(at + i * NZ * SHARD, NZ * SHARD)
            block = codes[q, i, :, :, GAB].astype(F32).reshape(NZ * SHARD, 768)
            flat[rows, 0:768] = block.astype(BF16)
            block = codes[q, i, :, :, GC].astype(F32).reshape(NZ * SHARD, 384)
            flat[rows, 768:WIDTH] = block.astype(BF16)
        spread = marks[q].astype(F32).reshape(NX, 1, SHARD, 128)
        code_ids = jnp.sum(spread * pick, axis=3, keepdims=True).reshape(SPAN, 1)
        logits = lax.dot_general(
            flat[pl.ds(at, SPAN), :], traces[...], (((1,), (1,)), ((), ())), preferred_element_type=F32
        )
        logits = logits * scale + shift
        same = code_ids == trace_ids
        raised = jnp.exp(jnp.where(same, logits, -logits))
        slope = jnp.where(same, -scale, scale) / (1.0 + raised)
        slopes[pl.ds(at, SPAN), :] = slope.astype(BF16)
        grad = jnp.dot(slopes[pl.ds(at, SPAN), :], traces[...], preferred_element_type=F32)
        parts[q] = grad.reshape(NX, NZ, SHARD, WIDTH).astype(BF16)

        @pl.when(j != 0)
        def _():
            for i in (2, 1, 3, 0):
                send_a1(j, i).start()

        for kind in (4, 5, 6):
            send_c1(j, kind).start()
        for k in range(1, NX):
            send_b1(j, k).start()
        for kind in (0, 1):
            send_c1(j, kind).start()

        @pl.when(step >= 2)
        def _():
            relay_c(block_at(step - 2))
            relay_b(block_at(step - 2))

            @pl.when(step == 3)
            def _():
                send_b2(1).start()

    relay_b(3)
    send_b2(3).start()
    relay_c(3)

    def trace_rows(first):
        return lax.dot_general(
            slopes[:, first : first + 256], flat[...], (((0,), (0,)), ((), ())), preferred_element_type=F32
        )

    for n in range(2):
        tg_send[n * 256 : n * 256 + 256, :] = trace_rows(ROWS + n * 256)
    d3 = remote(tg_send, tg_recv, dd, 2, other)
    d3.start()

    relay_b(2)
    send_b2(2).start()
    relay_c(2)
    a2 = []
    for i in (2, 1, 3, 0):
        for j in near:
            send_a1(j, i).wait_recv()
        total = parts[y, (x + i) % NX, :, :, A0:A1].astype(F32)
        for j in near:
            total = total + recv_a1[j - 1, i].astype(F32)
        sum_a[i] = total.astype(BF16)
        if i:
            a2.append(remote(sum_a.at[i], recv_a2.at[i - 1], rs, 26 + i, on_x(i)))
            a2[-1].start()
    for j in range(NY):
        for kind in range(4):
            send_c1(j, kind).wait_recv()
    for i in range(NY):
        total = parts[i, :, z, :, C0:C1].astype(F32)
        for kind in range(4):
            total = total + recv_c1[kind, i].astype(F32)
        sum_c[i] = total.astype(BF16)
    c2 = []
    for j, i in in_plane:
        c2.append(
            remote(sum_c.at[(y + j) % NY, (x + i) % NX], recv_c2.at[j * 4 + i], rsp, j * 4 + i, on_plane(j, i))
        )
        c2[-1].start()

    for j in near:
        send_b2(j).wait_recv()
    total = sum_b[0].astype(F32)
    for k in range(NY - 1):
        total = total + recv_b2[k].astype(F32)
    sum_ab[:, :, B0:B1] = total.astype(BF16)
    for copy in a2:
        copy.wait_recv()
    total = sum_a[0].astype(F32)
    for k in range(NX - 1):
        total = total + recv_a2[k].astype(F32)
    sum_ab[:, :, A0:A1] = total.astype(BF16)
    ab3 = []
    for k in near_z:
        ab3.append(remote(sum_ab.at[(z + k) % NZ], recv_ab3.at[k - 1], rs, 29 + k, on_z(k)))
        ab3[-1].start()

    for n in range(2):
        tg_own[n * 256 : n * 256 + 256, :] = trace_rows(n * 256)
    d3.wait()
    trace_out[...] = (tg_own[...] + tg_recv[...]).astype(BF16)

    for copy in c2:
        copy.wait_recv()
    total = sum_c[y, x].astype(F32)
    for j, i in in_plane:
        total = total + recv_c2[j * 4 + i].astype(F32)
    code_out[:, C0:C1] = total.astype(BF16)
    for copy in ab3:
        copy.wait_recv()
    total = sum_ab[z].astype(F32)
    for k in range(NZ - 1):
        total = total + recv_ab3[k].astype(F32)
    code_out[:, A0:B1] = total.astype(BF16)

    for copy in sent + c2 + a2 + ab3:
        copy.wait_send()
    for j in range(NY):
        if j:
            send_b2(j).wait_send()
            for i in range(NX):
                send_a1(j, i).wait_send()
        for k in near:
            send_b1(j, k).wait_send()
        for kind in range(7):
            send_c1(j, kind).wait_send()


def per_device(trace_emb, code_emb, trace_ids, code_ids, log_scale, bias):
    vmem = pl.BlockSpec(memory_space=pltpu.VMEM)
    dma = pltpu.SemaphoreType.DMA
    scratch = [
        pltpu.VMEM((SHARD, WIDTH), BF16),
        pltpu.VMEM((1, SHARD), jnp.int32),
        pltpu.VMEM((1, 1), F32),
        pltpu.VMEM((1, 1), F32),
        pltpu.VMEM((2 * ROWS, WIDTH), BF16),
        pltpu.VMEM((2, 1, ROWS), jnp.int32),
        pltpu.VMEM((NY, NX, NZ, SHARD, WIDE), BF16),
        pltpu.VMEM((NY, NX, SHARD, 128), BF16),
        pltpu.VMEM((PLANE, WIDTH), BF16),
        pltpu.VMEM((PLANE, 2 * ROWS), BF16),
        pltpu.VMEM((NY, NX, NZ, SHARD, WIDTH), BF16),
        pltpu.VMEM((NY - 1, NX, NZ, SHARD, A1 - A0), BF16),
        pltpu.VMEM((NX - 1, NY, NZ, SHARD, B1 - B0), BF16),
        pltpu.VMEM((7, NY, NX, SHARD, C1 - C0), BF16),
        pltpu.VMEM((2, NY, NX, SHARD, C1 - C0), BF16),
        pltpu.VMEM((NX, NZ, SHARD, A1 - A0), BF16),
        pltpu.VMEM((NY, NZ, SHARD, B1 - B0), BF16),
        pltpu.VMEM((NY, NX, SHARD, C1 - C0), BF16),
        pltpu.VMEM((NX - 1, NZ, SHARD, A1 - A0), BF16),
        pltpu.VMEM((NY - 1, NZ, SHARD, B1 - B0), BF16),
        pltpu.VMEM((NY * NX, SHARD, C1 - C0), BF16),
        pltpu.VMEM((NZ, SHARD, B1 - A0), BF16),
        pltpu.VMEM((NZ - 1, SHARD, B1 - A0), BF16),
        pltpu.VMEM((ROWS, WIDTH), F32),
        pltpu.VMEM((ROWS, WIDTH), F32),
        pltpu.VMEM((ROWS, WIDTH), F32),
        dma((6,)),
        dma((3,)),
        dma((3,)),
        dma((25,)),
        dma((25,)),
        dma((16,)),
        dma((16,)),
        dma((16,)),
        dma((16,)),
        dma((28,)),
        dma((28,)),
        dma((16,)),
        dma((16,)),
        dma((41,)),
        dma((41,)),
        dma((28,)),
        dma((28,)),
        dma((16,)),
        dma((16,)),
    ]
    return pl.pallas_call(
        kernel,
        out_shape=(pltpu.VMEM((ROWS, WIDTH), BF16), pltpu.VMEM((SHARD, WIDTH), BF16)),
        in_specs=[pl.BlockSpec(memory_space=pl.ANY)] * 6,
        out_specs=(vmem, vmem),
        scratch_shapes=scratch,
        compiler_params=pltpu.CompilerParams(
            collective_id=0, has_side_effects=True, vmem_limit_bytes=56 * 2**20
        ),
        name="contrast",
    )(
        trace_emb,
        code_emb,
        trace_ids.reshape(1, ROWS),
        code_ids.reshape(1, SHARD),
        log_scale.reshape(1, 1),
        bias.reshape(1, 1),
    )


def solution(mesh):
    placed = (
        P(("blk", "group"), None),
        P(("blk", "group"), None),
        P(("blk", "group")),
        P(("blk", "group")),
        P(),
        P(),
    )
    return jax.shard_map(
        per_device,
        mesh=mesh,
        in_specs=placed,
        out_specs=(P(("blk", "group"), None), P(("blk", "group"), None)),
        check_vma=False,
    )
```

```python
import jax
import jax.numpy as jnp
from jax import lax
from jax.experimental import pallas as pl
from jax.experimental.pallas import tpu as pltpu
from jax.sharding import PartitionSpec as P

MESH = pl.DeviceIdType.MESH
F32 = jnp.float32
BF16 = jnp.bfloat16

NY, NX, NZ = 4, 4, 8
SHARD = 8
WIDTH = 1152
ROWS = 512
A0, A1 = 0, 384
B0, B1 = 384, 768
C0, C1 = 768, 1152
GA = slice(0, 384)
GB = slice(384, 768)
GAB = slice(0, 768)
GM = slice(768, 896)
GABM = slice(0, 896)
GC = slice(896, 1280)
WIDE = 1280
SPAN = NX * NZ * SHARD
UP = (0, 1, 7, 2, 6, 3, 5, 4)
SLOT = tuple(UP.index(d) for d in range(NZ))
HALF = NZ // 2
PLANE = NY * SPAN


def place():
    blk = lax.axis_index("blk")
    group = lax.axis_index("group")
    x = (group // 16) * 2 + blk // 4
    return blk % 4, x, (group // 2) % NZ, group % 2


def device(y, x, z, core):
    return ((x % 2) * 4 + y, ((x // 2) * NZ + z) * 2 + core)


def remote(src, dst, sems, index, target):
    return pltpu.make_async_remote_copy(
        src_ref=src,
        dst_ref=dst,
        send_sem=sems[0].at[index],
        recv_sem=sems[1].at[index],
        device_id=target,
        device_id_type=MESH,
    )


def kernel(
    trace_ref, code_ref, tid_ref, cid_ref, scale_ref, shift_ref,
    trace_out, code_out,
    code_v, cid_v, scale_v, shift_v, traces, tids, codes, marks, flat, slopes, parts,
    recv_a1, recv_b1, recv_c1, sum_z, sum_a, sum_b, sum_c, recv_a2, recv_b2, recv_c2,
    sum_ab, recv_ab3, tg_own, tg_send, tg_recv,
    local, s_d, r_d, s_ag, r_ag, s_g3a, r_g3a, s_g3b, r_g3b, s_g3c, r_g3c, s_g1p, r_g1p, s_g2s, r_g2s, s_rs, r_rs, s_rsc, r_rsc, s_rsp, r_rsp,
):
    y, x, z, core = place()
    ag = (s_ag, r_ag)
    rs = (s_rs, r_rs)
    dd = (s_d, r_d)
    g3a, g3b, g3c = (s_g3a, r_g3a), (s_g3b, r_g3b), (s_g3c, r_g3c)
    g2s = (s_g2s, r_g2s)
    g1p, rsc, rsp = (s_g1p, r_g1p), (s_rsc, r_rsc), (s_rsp, r_rsp)

    def on_y(k):
        return device((y + k) % NY, x, z, core)

    def on_x(k):
        return device(y, (x + k) % NX, z, core)

    def on_z(k):
        return device(y, x, (z + k) % NZ, core)

    def on_plane(j, i):
        return device((y + j) % NY, (x + i) % NX, z, core)

    other = device(y, x, z, 1 - core)

    pairs = (
        (trace_ref, traces.at[0:ROWS]), (code_ref, code_v), (cid_ref, cid_v),
        (tid_ref, tids.at[0]), (scale_ref, scale_v), (shift_ref, shift_v),
    )
    fetch = [pltpu.make_async_copy(src, dst, local.at[n]) for n, (src, dst) in enumerate(pairs)]
    for n in (1, 2, 0, 3, 4, 5):
        fetch[n].start()

    barrier = pltpu.get_barrier_semaphore()
    in_plane = [(j, i) for j in (0, 1, 3, 2) for i in (0, 1, 3, 2) if (j, i) != (0, 0)]
    partners = [on_plane(j, i) for j, i in in_plane]
    partners += [on_z(k) for k in range(1, NZ)] + [other]
    for partner in partners:
        pl.semaphore_signal(barrier, inc=1, device_id=partner, device_id_type=MESH)

    fetch[1].wait()
    fetch[2].wait()
    spread = jnp.broadcast_to(cid_v[...], (SHARD, SHARD))
    row = lax.broadcasted_iota(jnp.int32, (SHARD, SHARD), 0)
    column = lax.broadcasted_iota(jnp.int32, (SHARD, SHARD), 1)
    ids = jnp.sum(jnp.where(row == column, spread, 0), axis=1, keepdims=True)
    high = (ids // 16).astype(F32)
    low = (ids % 16).astype(F32)
    lane = lax.broadcasted_iota(jnp.int32, (SHARD, 128), 1)
    tile = jnp.where(lane == 2 * z, high, jnp.where(lane == 2 * z + 1, low, 0.0)).astype(BF16)
    codes[y, x, 0, :, GAB] = code_v[:, 0:768]
    codes[y, x, 0, :, GM] = tile
    codes[y, x, 0, :, GC] = code_v[:, 768:WIDTH]
    pl.semaphore_wait(barrier, len(partners))

    near_z = (1, 7, 2, 6, 3, 5, 4)
    near = (1, 3, 2)
    sent = []

    def go(copy):
        copy.start()
        sent.append(copy)
        return copy

    g1 = {}
    for k in (1, 7, 6, 2, 5, 3, 4):
        source, target = codes.at[y, x, 0, :, GABM], codes.at[y, x, SLOT[NZ - k], :, GABM]
        g1[k] = go(remote(source, target, ag, k - 1, on_z(k)))
    ref = codes.at[y, x, 0, :, GC]
    g1c = {(j, i): go(remote(ref, ref, g1p, j * 4 + i, on_plane(j, i))) for j, i in in_plane}

    d1 = remote(trace_ref, traces.at[ROWS : 2 * ROWS], dd, 0, other)
    d2 = remote(tid_ref, tids.at[1], dd, 1, other)
    d1.start()
    d2.start()

    def gather_a(i, way, hop, half):
        step = 1 - 2 * way
        ref = codes.at[(y - step * (hop - 1)) % NY, (x - i) % NX, pl.ds(half * HALF, HALF), :, GA]
        return remote(ref, ref, g3a, ((half * 2 + way) * 4 + i) * 2 + hop - 1, on_y(step))

    def gather_b(j, way, hop, half):
        step = 1 - 2 * way
        ref = codes.at[(y - j) % NY, (x - step * (hop - 1)) % NX, pl.ds(half * HALF, HALF), :, GB]
        return remote(ref, ref, g3b, ((half * 2 + way) * 4 + j) * 2 + hop - 1, on_x(step))

    def gather_c(j, kind):
        start, step = ((0, 1), (0, -1), (0, 2), (0, -2), (-2, 1), (2, -1), (None, 2 - 4 * (j // 2)))[kind]
        if kind == 6:
            here, there = SLOT[6] + (j // 2) * (SLOT[2] - SLOT[6]), SLOT[4]
        else:
            here, there = SLOT[start % NZ], SLOT[(start - step) % NZ]
        row = (y - j) % NY
        return remote(codes.at[row, :, here, :, GC], codes.at[row, :, there, :, GC], g3c, j * 7 + kind, on_z(step))

    def pass_on(n, half):
        for gather in (gather_a, gather_b):
            gather(n, n // 2, 1, half).wait_recv()
            go(gather(n, n // 2, 2, half))

    def set_out(gather, n, half):
        for way in (0, 1):
            go(gather(n, way, 1, half))

    def set_out_both(n, half):
        if n:
            g2a[half, n].wait_recv()
        set_out(gather_a, n, half)
        if n:
            g2b[half, n].wait_recv()
        set_out(gather_b, n, half)

    g2a, g2b = {}, {}

    def spread_both(half):
        part = pl.ds(half * HALF, HALF)
        for k in near:
            ref = codes.at[y, x, part, :, GA]
            g2a[half, k] = go(remote(ref, ref, g2s, half * 6 + k - 1, on_x(k)))
            ref = codes.at[y, x, part, :, GB]
            g2b[half, k] = go(remote(ref, ref, g2s, half * 6 + 2 + k, on_y(k)))
        set_out_both(0, half)

    def set_out_c(j):
        for i in near if j == 0 else (0, 1, 3, 2):
            g1c[j, i].wait_recv()
        for kind in (2, 3, 0, 1):
            go(gather_c(j, kind))

    def pass_on_c(j):
        gather_c(j, 2).wait_recv()
        go(gather_c(j, 4))
        if j < 2:
            go(gather_c(j, 6))
        gather_c(j, 3).wait_recv()
        go(gather_c(j, 5))
        if j >= 2:
            go(gather_c(j, 6))

    set_out_c(0)
    for k in (1, 7, 6):
        g1[k].wait_recv()
    spread_both(0)
    set_out_c(1)
    set_out_c(3)
    for k in (2, 5, 3, 4):
        g1[k].wait_recv()
    spread_both(1)
    set_out_c(2)
    marks[y, x] = jnp.sum(codes[y, x, :, :, GM].astype(F32), axis=0).astype(BF16)
    ref = marks.at[y, x]
    m2 = [go(remote(ref, ref, ag, 18 + k, on_x(k))) for k in near]
    set_out_both(1, 0)
    set_out_both(3, 0)
    pass_on_c(0)
    pass_on(0, 0)
    set_out_both(2, 0)
    set_out_both(1, 1)
    set_out_both(3, 1)
    pass_on(0, 1)
    set_out_both(2, 1)
    pass_on_c(1)
    for copy in m2:
        copy.wait_recv()
    ref = marks.at[y]
    m3 = [go(remote(ref, ref, ag, 21 + k, on_y(k))) for k in near]
    pass_on(3, 0)
    pass_on(1, 0)
    pass_on_c(3)
    pass_on(2, 0)
    pass_on(3, 1)
    pass_on(1, 1)
    pass_on_c(2)
    pass_on(2, 1)
    for copy in m3:
        copy.wait_recv()
    for n in (0, 3, 4, 5):
        fetch[n].wait()
    d1.wait()
    d2.wait()

    scale = jnp.exp(scale_v[...])
    shift = shift_v[...]
    trace_ids = jnp.concatenate([tids[0], tids[1]], axis=1).astype(F32)

    lane = lax.broadcasted_iota(jnp.int32, (1, NZ, 1, 128), 3)
    slot = lax.broadcasted_iota(jnp.int32, (1, NZ, 1, 128), 1)
    owner = jnp.zeros((1, NZ, 1, 128), jnp.int32)
    for n, up in enumerate(UP):
        owner = jnp.where(slot == n, (z + up) % NZ, owner)
    pick = jnp.where(lane == 2 * owner, 16.0, jnp.where(lane == 2 * owner + 1, 1.0, 0.0))

    def send_a1(j, i):
        q = (y - j) % NY
        return remote(
            parts.at[q, (x + i) % NX, :, :, A0:A1], recv_a1.at[j - 1, i], rs, (j - 1) * 4 + i, on_y(-j)
        )

    def send_b1(j, k):
        q = (y - j) % NY
        return remote(
            parts.at[q, (x + k) % NX, :, :, B0:B1], recv_b1.at[k - 1, j], rs, 12 + j * 3 + k - 1, on_x(k)
        )

    def send_b2(j):
        return remote(sum_b.at[j], recv_b2.at[j - 1], rs, 23 + j, on_y(-j))

    def relay_b(j):
        for k in near:
            send_b1(j, k).wait_recv()
        total = parts[(y - j) % NY, x, :, :, B0:B1].astype(F32)
        for k in near:
            total = total + recv_b1[k - 1, j].astype(F32)
        sum_b[j] = total.astype(BF16)

    def send_c1(j, kind):
        q = (y - j) % NY
        half = 2 - 4 * (j // 2)
        if kind in (2, 3):
            source = sum_z.at[kind - 2, q]
        else:
            away = (1, -1, None, None, 3, -3, 4)[kind]
            source = parts.at[q, :, SLOT[away % NZ], :, C0:C1]
        step = (1, -1, 2, -2, 1, -1, half)[kind]
        return remote(source, recv_c1.at[kind, q], rsc, j * 7 + kind, on_z(step))

    def relay_c(j):
        q = (y - j) % NY
        for kind in (4, 5, 6):
            send_c1(j, kind).wait_recv()
        upper = jnp.where(j < 2, 1.0, 0.0)
        middle = recv_c1[6, q].astype(F32)
        total = parts[q, :, SLOT[2], :, C0:C1].astype(F32) + recv_c1[4, q].astype(F32) + upper * middle
        sum_z[0, q] = total.astype(BF16)
        total = parts[q, :, SLOT[6], :, C0:C1].astype(F32) + recv_c1[5, q].astype(F32) + (1.0 - upper) * middle
        sum_z[1, q] = total.astype(BF16)
        send_c1(j, 2).start()
        send_c1(j, 3).start()

    def block_at(step):
        return (step % 2) * 2 + step // 2

    @pl.loop(0, NY)
    def _(step):
        j = block_at(step)
        q = (y - j) % NY

        for half in (0, 1):

            @pl.when(j == 1)
            def _():
                gather_a(2, 0, 1, half).wait_recv()
                gather_a(3, 0, 1, half).wait_recv()

            @pl.when(j == 3)
            def _():
                gather_a(0, 1, 1, half).wait_recv()
                gather_a(1, 1, 1, half).wait_recv()

            @pl.when(j == 2)
            def _():
                for i in range(NX):
                    gather_a(i, i // 2, 2, half).wait_recv()

            gather_b(j, 1 - j // 2, 1, half).wait_recv()
            gather_b(j, j // 2, 2, half).wait_recv()
        for kind in (0, 1, 4, 5, 6):
            gather_c(j, kind).wait_recv()
        at = pl.multiple_of(q * SPAN, SPAN)
        for i in range(NX):
            rows = pl.ds(at + i * NZ * SHARD, NZ * SHARD)
            block = codes[q, i, :, :, GAB].astype(F32).reshape(NZ * SHARD, 768)
            flat[rows, 0:768] = block.astype(BF16)
            block = codes[q, i, :, :, GC].astype(F32).reshape(NZ * SHARD, 384)
            flat[rows, 768:WIDTH] = block.astype(BF16)
        spread = marks[q].astype(F32).reshape(NX, 1, SHARD, 128)
        code_ids = jnp.sum(spread * pick, axis=3, keepdims=True).reshape(SPAN, 1)
        logits = lax.dot_general(
            flat[pl.ds(at, SPAN), :], traces[...], (((1,), (1,)), ((), ())), preferred_element_type=F32
        )
        logits = logits * scale + shift
        same = code_ids == trace_ids
        raised = jnp.exp(jnp.where(same, logits, -logits))
        slope = jnp.where(same, -scale, scale) / (1.0 + raised)
        slopes[pl.ds(at, SPAN), :] = slope.astype(BF16)
        grad = jnp.dot(slopes[pl.ds(at, SPAN), :], traces[...], preferred_element_type=F32)
        parts[q] = grad.reshape(NX, NZ, SHARD, WIDTH).astype(BF16)

        @pl.when(j != 0)
        def _():
            for i in (2, 1, 3, 0):
                send_a1(j, i).start()

        for kind in (4, 5, 6):
            send_c1(j, kind).start()
        for k in range(1, NX):
            send_b1(j, k).start()
        for kind in (0, 1):
            send_c1(j, kind).start()

        @pl.when(step >= 2)
        def _():
            relay_c(block_at(step - 2))
            relay_b(block_at(step - 2))

            @pl.when(step == 3)
            def _():
                send_b2(2).start()

    relay_b(1)
    send_b2(1).start()
    relay_c(1)

    def trace_rows(first):
        return lax.dot_general(
            slopes[:, first : first + 256], flat[...], (((0,), (0,)), ((), ())), preferred_element_type=F32
        )

    def trace_to_other(n):
        rows = pl.ds(n * 256, 256)
        tg_send[rows, :] = trace_rows(ROWS + n * 256)
        copy = remote(tg_send.at[rows], tg_recv.at[rows], dd, 2 + n, other)
        copy.start()
        return copy

    d3 = [trace_to_other(0)]

    relay_b(3)
    send_b2(3).start()
    a2 = []

    def sum_up_a(i):
        for j in near:
            send_a1(j, i).wait_recv()
        total = parts[y, (x + i) % NX, :, :, A0:A1].astype(F32)
        for j in near:
            total = total + recv_a1[j - 1, i].astype(F32)
        sum_a[i] = total.astype(BF16)
        if i:
            a2.append(remote(sum_a.at[i], recv_a2.at[i - 1], rs, 26 + i, on_x(i)))
            a2[-1].start()

    sum_up_a(2)
    relay_c(3)
    sum_up_a(1)
    sum_up_a(3)
    d3.append(trace_to_other(1))
    sum_up_a(0)

    for j in near:
        send_b2(j).wait_recv()
    total = sum_b[0].astype(F32)
    for k in range(NY - 1):
        total = total + recv_b2[k].astype(F32)
    sum_ab[:, :, B0:B1] = total.astype(BF16)
    for copy in a2:
        copy.wait_recv()
    total = sum_a[0].astype(F32)
    for k in range(NX - 1):
        total = total + recv_a2[k].astype(F32)
    sum_ab[:, :, A0:A1] = total.astype(BF16)
    ab3 = []
    for k in near_z:
        ab3.append(remote(sum_ab.at[SLOT[k]], recv_ab3.at[k - 1], rs, 29 + k, on_z(k)))
        ab3[-1].start()

    for j in range(NY):
        for kind in range(4):
            send_c1(j, kind).wait_recv()
    for i in range(NY):
        total = parts[i, :, 0, :, C0:C1].astype(F32)
        for kind in range(4):
            total = total + recv_c1[kind, i].astype(F32)
        sum_c[i] = total.astype(BF16)
    c2 = []
    for j, i in in_plane:
        c2.append(
            remote(sum_c.at[(y + j) % NY, (x + i) % NX], recv_c2.at[j * 4 + i], rsp, j * 4 + i, on_plane(j, i))
        )
        c2[-1].start()

    for n in range(2):
        tg_own[n * 256 : n * 256 + 256, :] = trace_rows(n * 256)
    for copy in d3:
        copy.wait_recv()
    trace_out[...] = (tg_own[...] + tg_recv[...]).astype(BF16)

    for copy in sent + a2 + d3:
        copy.wait_send()
    for j in range(NY):
        if j:
            send_b2(j).wait_send()
            for i in range(NX):
                send_a1(j, i).wait_send()
        for k in near:
            send_b1(j, k).wait_send()
        for kind in range(7):
            send_c1(j, kind).wait_send()

    for copy in c2:
        copy.wait_recv()
    total = sum_c[y, x].astype(F32)
    for j, i in in_plane:
        total = total + recv_c2[j * 4 + i].astype(F32)
    code_out[:, C0:C1] = total.astype(BF16)
    for copy in ab3:
        copy.wait_recv()
    total = sum_ab[0].astype(F32)
    for k in range(NZ - 1):
        total = total + recv_ab3[k].astype(F32)
    code_out[:, A0:B1] = total.astype(BF16)

    for copy in c2 + ab3:
        copy.wait_send()


def per_device(trace_emb, code_emb, trace_ids, code_ids, log_scale, bias):
    vmem = pl.BlockSpec(memory_space=pltpu.VMEM)
    dma = pltpu.SemaphoreType.DMA
    scratch = [
        pltpu.VMEM((SHARD, WIDTH), BF16),
        pltpu.VMEM((1, SHARD), jnp.int32),
        pltpu.VMEM((1, 1), F32),
        pltpu.VMEM((1, 1), F32),
        pltpu.VMEM((2 * ROWS, WIDTH), BF16),
        pltpu.VMEM((2, 1, ROWS), jnp.int32),
        pltpu.VMEM((NY, NX, NZ, SHARD, WIDE), BF16),
        pltpu.VMEM((NY, NX, SHARD, 128), BF16),
        pltpu.VMEM((PLANE, WIDTH), BF16),
        pltpu.VMEM((PLANE, 2 * ROWS), BF16),
        pltpu.VMEM((NY, NX, NZ, SHARD, WIDTH), BF16),
        pltpu.VMEM((NY - 1, NX, NZ, SHARD, A1 - A0), BF16),
        pltpu.VMEM((NX - 1, NY, NZ, SHARD, B1 - B0), BF16),
        pltpu.VMEM((7, NY, NX, SHARD, C1 - C0), BF16),
        pltpu.VMEM((2, NY, NX, SHARD, C1 - C0), BF16),
        pltpu.VMEM((NX, NZ, SHARD, A1 - A0), BF16),
        pltpu.VMEM((NY, NZ, SHARD, B1 - B0), BF16),
        pltpu.VMEM((NY, NX, SHARD, C1 - C0), BF16),
        pltpu.VMEM((NX - 1, NZ, SHARD, A1 - A0), BF16),
        pltpu.VMEM((NY - 1, NZ, SHARD, B1 - B0), BF16),
        pltpu.VMEM((NY * NX, SHARD, C1 - C0), BF16),
        pltpu.VMEM((NZ, SHARD, B1 - A0), BF16),
        pltpu.VMEM((NZ - 1, SHARD, B1 - A0), BF16),
        pltpu.VMEM((ROWS, WIDTH), F32),
        pltpu.VMEM((ROWS, WIDTH), F32),
        pltpu.VMEM((ROWS, WIDTH), F32),
        dma((6,)),
        dma((4,)),
        dma((4,)),
        dma((25,)),
        dma((25,)),
        dma((32,)),
        dma((32,)),
        dma((32,)),
        dma((32,)),
        dma((28,)),
        dma((28,)),
        dma((16,)),
        dma((16,)),
        dma((12,)),
        dma((12,)),
        dma((41,)),
        dma((41,)),
        dma((28,)),
        dma((28,)),
        dma((16,)),
        dma((16,)),
    ]
    return pl.pallas_call(
        kernel,
        out_shape=(pltpu.VMEM((ROWS, WIDTH), BF16), pltpu.VMEM((SHARD, WIDTH), BF16)),
        in_specs=[pl.BlockSpec(memory_space=pl.ANY)] * 6,
        out_specs=(vmem, vmem),
        scratch_shapes=scratch,
        compiler_params=pltpu.CompilerParams(
            collective_id=0, has_side_effects=True, vmem_limit_bytes=56 * 2**20
        ),
        name="contrast",
    )(
        trace_emb,
        code_emb,
        trace_ids.reshape(1, ROWS),
        code_ids.reshape(1, SHARD),
        log_scale.reshape(1, 1),
        bias.reshape(1, 1),
    )


def solution(mesh):
    placed = (
        P(("blk", "group"), None),
        P(("blk", "group"), None),
        P(("blk", "group")),
        P(("blk", "group")),
        P(),
        P(),
    )
    return jax.shard_map(
        per_device,
        mesh=mesh,
        in_specs=placed,
        out_specs=(P(("blk", "group"), None), P(("blk", "group"), None)),
        check_vma=False,
    )
```

```python
import jax
import jax.numpy as jnp
from jax import lax
from jax.experimental import pallas as pl
from jax.experimental.pallas import tpu as pltpu
from jax.sharding import PartitionSpec as P

MESH = pl.DeviceIdType.MESH
F32 = jnp.float32
BF16 = jnp.bfloat16

NY, NX, NZ = 4, 4, 8
SHARD = 8
WIDTH = 1152
ROWS = 512
A0, A1 = 0, 384
B0, B1 = 384, 768
C0, C1 = 768, 1152
GA = slice(0, 384)
GB = slice(384, 768)
GAB = slice(0, 768)
GM = slice(768, 896)
GABM = slice(0, 896)
GC = slice(896, 1280)
WIDE = 1280
SPAN = NX * NZ * SHARD
UP = (0, 1, 7, 2, 6, 3, 5, 4)
SLOT = tuple(UP.index(d) for d in range(NZ))
HALF = NZ // 2
PLANE = NY * SPAN


def place():
    blk = lax.axis_index("blk")
    group = lax.axis_index("group")
    x = (group // 16) * 2 + blk // 4
    return blk % 4, x, (group // 2) % NZ, group % 2


def device(y, x, z, core):
    return ((x % 2) * 4 + y, ((x // 2) * NZ + z) * 2 + core)


def remote(src, dst, sems, index, target):
    return pltpu.make_async_remote_copy(
        src_ref=src,
        dst_ref=dst,
        send_sem=sems[0].at[index],
        recv_sem=sems[1].at[index],
        device_id=target,
        device_id_type=MESH,
    )


def kernel(
    trace_ref, code_ref, tid_ref, cid_ref, scale_ref, shift_ref,
    trace_out, code_out,
    code_v, cid_v, scale_v, shift_v, traces, tids, codes, marks, flat, slopes, parts,
    recv_a1, recv_b1, recv_c1, sum_z, sum_a, sum_b, sum_c, recv_a2, recv_b2, recv_c2,
    sum_ab, recv_ab3, tg_own, tg_send, tg_recv,
    local, s_d, r_d, s_ag, r_ag, s_g3a, r_g3a, s_g3b, r_g3b, s_g3c, r_g3c, s_g1p, r_g1p, s_g2s, r_g2s, s_rs, r_rs, s_rsc, r_rsc, s_rsp, r_rsp,
):
    y, x, z, core = place()
    ag = (s_ag, r_ag)
    rs = (s_rs, r_rs)
    dd = (s_d, r_d)
    g3a, g3b, g3c = (s_g3a, r_g3a), (s_g3b, r_g3b), (s_g3c, r_g3c)
    g2s = (s_g2s, r_g2s)
    g1p, rsc, rsp = (s_g1p, r_g1p), (s_rsc, r_rsc), (s_rsp, r_rsp)

    def on_y(k):
        return device((y + k) % NY, x, z, core)

    def on_x(k):
        return device(y, (x + k) % NX, z, core)

    def on_z(k):
        return device(y, x, (z + k) % NZ, core)

    def on_plane(j, i):
        return device((y + j) % NY, (x + i) % NX, z, core)

    other = device(y, x, z, 1 - core)

    pairs = (
        (trace_ref, traces.at[0:ROWS]), (code_ref, code_v), (cid_ref, cid_v),
        (tid_ref, tids.at[0]), (scale_ref, scale_v), (shift_ref, shift_v),
    )
    fetch = [pltpu.make_async_copy(src, dst, local.at[n]) for n, (src, dst) in enumerate(pairs)]

    barrier = pltpu.get_barrier_semaphore()
    in_plane = [(j, i) for j in (0, 1, 3, 2) for i in (0, 1, 3, 2) if (j, i) != (0, 0)]
    partners = [on_plane(j, i) for j, i in in_plane]
    partners += [on_z(k) for k in range(1, NZ)] + [other]
    for partner in partners:
        pl.semaphore_signal(barrier, inc=1, device_id=partner, device_id_type=MESH)
    for n in (1, 2, 0, 3, 4, 5):
        fetch[n].start()

    fetch[1].wait()
    fetch[2].wait()
    spread = jnp.broadcast_to(cid_v[...], (SHARD, SHARD))
    row = lax.broadcasted_iota(jnp.int32, (SHARD, SHARD), 0)
    column = lax.broadcasted_iota(jnp.int32, (SHARD, SHARD), 1)
    ids = jnp.sum(jnp.where(row == column, spread, 0), axis=1, keepdims=True)
    high = (ids // 16).astype(F32)
    low = (ids % 16).astype(F32)
    lane = lax.broadcasted_iota(jnp.int32, (SHARD, 128), 1)
    tile = jnp.where(lane == 2 * z, high, jnp.where(lane == 2 * z + 1, low, 0.0)).astype(BF16)
    codes[y, x, 0, :, GAB] = code_v[:, 0:768]
    codes[y, x, 0, :, GM] = tile
    codes[y, x, 0, :, GC] = code_v[:, 768:WIDTH]
    pl.semaphore_wait(barrier, len(partners))

    near_z = (1, 7, 2, 6, 3, 5, 4)
    near = (1, 3, 2)
    sent = []

    def go(copy):
        copy.start()
        sent.append(copy)
        return copy

    g1 = {}
    for k in (1, 7, 6, 2, 5, 3, 4):
        source, target = codes.at[y, x, 0, :, GABM], codes.at[y, x, SLOT[NZ - k], :, GABM]
        g1[k] = go(remote(source, target, ag, k - 1, on_z(k)))
    ref = codes.at[y, x, 0, :, GC]
    g1c = {(j, i): go(remote(ref, ref, g1p, j * 4 + i, on_plane(j, i))) for j, i in in_plane}

    d1 = remote(trace_ref, traces.at[ROWS : 2 * ROWS], dd, 0, other)
    d2 = remote(tid_ref, tids.at[1], dd, 1, other)
    d1.start()
    d2.start()

    def gather_a(i, way, hop, half):
        step = 1 - 2 * way
        ref = codes.at[(y - step * (hop - 1)) % NY, (x - i) % NX, pl.ds(half * HALF, HALF), :, GA]
        return remote(ref, ref, g3a, ((half * 2 + way) * 4 + i) * 2 + hop - 1, on_y(step))

    def gather_b(j, way, hop, half):
        step = 1 - 2 * way
        ref = codes.at[(y - j) % NY, (x - step * (hop - 1)) % NX, pl.ds(half * HALF, HALF), :, GB]
        return remote(ref, ref, g3b, ((half * 2 + way) * 4 + j) * 2 + hop - 1, on_x(step))

    def gather_c(j, kind):
        start, step = ((0, 1), (0, -1), (0, 2), (0, -2), (-2, 1), (2, -1), (None, 2 - 4 * (j // 2)))[kind]
        if kind == 6:
            here, there = SLOT[6] + (j // 2) * (SLOT[2] - SLOT[6]), SLOT[4]
        else:
            here, there = SLOT[start % NZ], SLOT[(start - step) % NZ]
        row = (y - j) % NY
        return remote(codes.at[row, :, here, :, GC], codes.at[row, :, there, :, GC], g3c, j * 7 + kind, on_z(step))

    def pass_on(n, half):
        for gather in (gather_a, gather_b):
            gather(n, n // 2, 1, half).wait_recv()
            go(gather(n, n // 2, 2, half))

    def set_out(gather, n, half):
        for way in (0, 1):
            go(gather(n, way, 1, half))

    def set_out_both(n, half):
        if n:
            g2a[half, n].wait_recv()
        set_out(gather_a, n, half)
        if n:
            g2b[half, n].wait_recv()
        set_out(gather_b, n, half)

    g2a, g2b = {}, {}

    def spread_both(half):
        part = pl.ds(half * HALF, HALF)
        for k in near:
            ref = codes.at[y, x, part, :, GA]
            g2a[half, k] = go(remote(ref, ref, g2s, half * 6 + k - 1, on_x(k)))
            ref = codes.at[y, x, part, :, GB]
            g2b[half, k] = go(remote(ref, ref, g2s, half * 6 + 2 + k, on_y(k)))
        set_out_both(0, half)

    def set_out_c(j):
        for i in near if j == 0 else (0, 1, 3, 2):
            g1c[j, i].wait_recv()
        for kind in (2, 3, 0, 1):
            go(gather_c(j, kind))

    def pass_on_c(j):
        gather_c(j, 2).wait_recv()
        go(gather_c(j, 4))
        if j < 2:
            go(gather_c(j, 6))
        gather_c(j, 3).wait_recv()
        go(gather_c(j, 5))
        if j >= 2:
            go(gather_c(j, 6))

    set_out_c(0)
    for k in (1, 7, 6):
        g1[k].wait_recv()
    spread_both(0)
    set_out_c(1)
    set_out_c(3)
    for k in (2, 5, 3, 4):
        g1[k].wait_recv()
    spread_both(1)
    set_out_c(2)
    marks[y, x] = jnp.sum(codes[y, x, :, :, GM].astype(F32), axis=0).astype(BF16)
    ref = marks.at[y, x]
    m2 = [go(remote(ref, ref, ag, 18 + k, on_x(k))) for k in near]
    pass_on(0, 0)
    set_out_both(1, 0)
    set_out_both(3, 0)
    pass_on_c(0)
    set_out_both(2, 0)
    set_out_both(1, 1)
    set_out_both(3, 1)
    pass_on(0, 1)
    set_out_both(2, 1)
    pass_on_c(1)
    for copy in m2:
        copy.wait_recv()
    ref = marks.at[y]
    m3 = [go(remote(ref, ref, ag, 21 + k, on_y(k))) for k in near]
    pass_on(3, 0)
    pass_on(1, 0)
    pass_on_c(3)
    pass_on(2, 0)
    pass_on(3, 1)
    pass_on(1, 1)
    pass_on_c(2)
    pass_on(2, 1)
    for copy in m3:
        copy.wait_recv()
    for n in (0, 3, 4, 5):
        fetch[n].wait()
    d1.wait()
    d2.wait()

    scale = jnp.exp(scale_v[...])
    shift = shift_v[...]
    trace_ids = jnp.concatenate([tids[0], tids[1]], axis=1).astype(F32)

    lane = lax.broadcasted_iota(jnp.int32, (1, NZ, 1, 128), 3)
    slot = lax.broadcasted_iota(jnp.int32, (1, NZ, 1, 128), 1)
    owner = jnp.zeros((1, NZ, 1, 128), jnp.int32)
    for n, up in enumerate(UP):
        owner = jnp.where(slot == n, (z + up) % NZ, owner)
    pick = jnp.where(lane == 2 * owner, 16.0, jnp.where(lane == 2 * owner + 1, 1.0, 0.0))

    def send_a1(j, i):
        q = (y - j) % NY
        return remote(
            parts.at[q, (x + i) % NX, :, :, A0:A1], recv_a1.at[j - 1, i], rs, (j - 1) * 4 + i, on_y(-j)
        )

    def send_b1(j, k):
        q = (y - j) % NY
        return remote(
            parts.at[q, (x + k) % NX, :, :, B0:B1], recv_b1.at[k - 1, j], rs, 12 + j * 3 + k - 1, on_x(k)
        )

    def send_b2(j):
        return remote(sum_b.at[j], recv_b2.at[j - 1], rs, 23 + j, on_y(-j))

    def relay_b(j):
        for k in near:
            send_b1(j, k).wait_recv()
        total = parts[(y - j) % NY, x, :, :, B0:B1].astype(F32)
        for k in near:
            total = total + recv_b1[k - 1, j].astype(F32)
        sum_b[j] = total.astype(BF16)

    def send_c1(j, kind):
        q = (y - j) % NY
        half = 2 - 4 * (j // 2)
        if kind in (2, 3):
            source = sum_z.at[kind - 2, q]
        else:
            away = (1, -1, None, None, 3, -3, 4)[kind]
            source = parts.at[q, :, SLOT[away % NZ], :, C0:C1]
        step = (1, -1, 2, -2, 1, -1, half)[kind]
        return remote(source, recv_c1.at[kind, q], rsc, j * 7 + kind, on_z(step))

    def relay_c(j):
        q = (y - j) % NY
        for kind in (4, 5, 6):
            send_c1(j, kind).wait_recv()
        upper = jnp.where(j < 2, 1.0, 0.0)
        middle = recv_c1[6, q].astype(F32)
        total = parts[q, :, SLOT[2], :, C0:C1].astype(F32) + recv_c1[4, q].astype(F32) + upper * middle
        sum_z[0, q] = total.astype(BF16)
        total = parts[q, :, SLOT[6], :, C0:C1].astype(F32) + recv_c1[5, q].astype(F32) + (1.0 - upper) * middle
        sum_z[1, q] = total.astype(BF16)
        send_c1(j, 2).start()
        send_c1(j, 3).start()

    def block_at(step):
        return (step % 2) * 2 + step // 2

    @pl.loop(0, NY)
    def _(step):
        j = block_at(step)
        q = (y - j) % NY

        for half in (0, 1):

            @pl.when(j == 1)
            def _():
                gather_a(2, 0, 1, half).wait_recv()
                gather_a(3, 0, 1, half).wait_recv()

            @pl.when(j == 3)
            def _():
                gather_a(0, 1, 1, half).wait_recv()
                gather_a(1, 1, 1, half).wait_recv()

            @pl.when(j == 2)
            def _():
                for i in range(NX):
                    gather_a(i, i // 2, 2, half).wait_recv()

            gather_b(j, 1 - j // 2, 1, half).wait_recv()
            gather_b(j, j // 2, 2, half).wait_recv()
        for kind in (0, 1, 4, 5, 6):
            gather_c(j, kind).wait_recv()
        at = pl.multiple_of(q * SPAN, SPAN)
        for i in range(NX):
            rows = pl.ds(at + i * NZ * SHARD, NZ * SHARD)
            block = codes[q, i, :, :, GAB].astype(F32).reshape(NZ * SHARD, 768)
            flat[rows, 0:768] = block.astype(BF16)
            block = codes[q, i, :, :, GC].astype(F32).reshape(NZ * SHARD, 384)
            flat[rows, 768:WIDTH] = block.astype(BF16)
        spread = marks[q].astype(F32).reshape(NX, 1, SHARD, 128)
        code_ids = jnp.sum(spread * pick, axis=3, keepdims=True).reshape(SPAN, 1)
        logits = lax.dot_general(
            flat[pl.ds(at, SPAN), :], traces[...], (((1,), (1,)), ((), ())), preferred_element_type=F32
        )
        logits = logits * scale + shift
        same = code_ids == trace_ids
        raised = jnp.exp(jnp.where(same, logits, -logits))
        slope = jnp.where(same, -scale, scale) / (1.0 + raised)
        slopes[pl.ds(at, SPAN), :] = slope.astype(BF16)
        grad = jnp.dot(slopes[pl.ds(at, SPAN), :], traces[...], preferred_element_type=F32)
        parts[q] = grad.reshape(NX, NZ, SHARD, WIDTH).astype(BF16)

        @pl.when(j != 0)
        def _():
            for i in (2, 1, 3, 0):
                send_a1(j, i).start()

        for kind in (4, 5, 6):
            send_c1(j, kind).start()
        for k in range(1, NX):
            send_b1(j, k).start()
        for kind in (0, 1):
            send_c1(j, kind).start()

        @pl.when(step >= 2)
        def _():
            relay_c(block_at(step - 2))
            relay_b(block_at(step - 2))

            @pl.when(step == 3)
            def _():
                send_b2(2).start()

    relay_b(1)
    send_b2(1).start()
    relay_c(1)

    def trace_rows(first):
        return lax.dot_general(
            slopes[:, first : first + 256], flat[...], (((0,), (0,)), ((), ())), preferred_element_type=F32
        )

    def trace_to_other(n):
        rows = pl.ds(n * 256, 256)
        tg_send[rows, :] = trace_rows(ROWS + n * 256)
        copy = remote(tg_send.at[rows], tg_recv.at[rows], dd, 2 + n, other)
        copy.start()
        return copy

    d3 = [trace_to_other(0)]

    relay_b(3)
    send_b2(3).start()
    a2 = []

    def sum_up_a(i):
        for j in near:
            send_a1(j, i).wait_recv()
        total = parts[y, (x + i) % NX, :, :, A0:A1].astype(F32)
        for j in near:
            total = total + recv_a1[j - 1, i].astype(F32)
        sum_a[i] = total.astype(BF16)
        if i:
            a2.append(remote(sum_a.at[i], recv_a2.at[i - 1], rs, 26 + i, on_x(i)))
            a2[-1].start()

    sum_up_a(2)
    relay_c(3)
    sum_up_a(1)
    sum_up_a(3)
    d3.append(trace_to_other(1))
    sum_up_a(0)

    for j in near:
        send_b2(j).wait_recv()
    total = sum_b[0].astype(F32)
    for k in range(NY - 1):
        total = total + recv_b2[k].astype(F32)
    sum_ab[:, :, B0:B1] = total.astype(BF16)
    for copy in a2:
        copy.wait_recv()
    total = sum_a[0].astype(F32)
    for k in range(NX - 1):
        total = total + recv_a2[k].astype(F32)
    sum_ab[:, :, A0:A1] = total.astype(BF16)
    ab3 = []
    for k in near_z:
        ab3.append(remote(sum_ab.at[SLOT[k]], recv_ab3.at[k - 1], rs, 29 + k, on_z(k)))
        ab3[-1].start()

    for j in range(NY):
        for kind in range(4):
            send_c1(j, kind).wait_recv()
    for i in range(NY):
        total = parts[i, :, 0, :, C0:C1].astype(F32)
        for kind in range(4):
            total = total + recv_c1[kind, i].astype(F32)
        sum_c[i] = total.astype(BF16)
    c2 = []
    for j, i in in_plane:
        c2.append(
            remote(sum_c.at[(y + j) % NY, (x + i) % NX], recv_c2.at[j * 4 + i], rsp, j * 4 + i, on_plane(j, i))
        )
        c2[-1].start()

    for n in range(2):
        tg_own[n * 256 : n * 256 + 256, :] = trace_rows(n * 256)
    for copy in d3:
        copy.wait_recv()
    trace_out[...] = (tg_own[...] + tg_recv[...]).astype(BF16)

    for copy in sent + a2 + d3:
        copy.wait_send()
    for j in range(NY):
        if j:
            send_b2(j).wait_send()
            for i in range(NX):
                send_a1(j, i).wait_send()
        for k in near:
            send_b1(j, k).wait_send()
        for kind in range(7):
            send_c1(j, kind).wait_send()

    for copy in c2:
        copy.wait_recv()
    total = sum_c[y, x].astype(F32)
    for j, i in in_plane:
        total = total + recv_c2[j * 4 + i].astype(F32)
    code_out[:, C0:C1] = total.astype(BF16)
    for copy in ab3:
        copy.wait_recv()
    total = sum_ab[0].astype(F32)
    for k in range(NZ - 1):
        total = total + recv_ab3[k].astype(F32)
    code_out[:, A0:B1] = total.astype(BF16)

    for copy in c2 + ab3:
        copy.wait_send()


def per_device(trace_emb, code_emb, trace_ids, code_ids, log_scale, bias):
    vmem = pl.BlockSpec(memory_space=pltpu.VMEM)
    dma = pltpu.SemaphoreType.DMA
    scratch = [
        pltpu.VMEM((SHARD, WIDTH), BF16),
        pltpu.VMEM((1, SHARD), jnp.int32),
        pltpu.VMEM((1, 1), F32),
        pltpu.VMEM((1, 1), F32),
        pltpu.VMEM((2 * ROWS, WIDTH), BF16),
        pltpu.VMEM((2, 1, ROWS), jnp.int32),
        pltpu.VMEM((NY, NX, NZ, SHARD, WIDE), BF16),
        pltpu.VMEM((NY, NX, SHARD, 128), BF16),
        pltpu.VMEM((PLANE, WIDTH), BF16),
        pltpu.VMEM((PLANE, 2 * ROWS), BF16),
        pltpu.VMEM((NY, NX, NZ, SHARD, WIDTH), BF16),
        pltpu.VMEM((NY - 1, NX, NZ, SHARD, A1 - A0), BF16),
        pltpu.VMEM((NX - 1, NY, NZ, SHARD, B1 - B0), BF16),
        pltpu.VMEM((7, NY, NX, SHARD, C1 - C0), BF16),
        pltpu.VMEM((2, NY, NX, SHARD, C1 - C0), BF16),
        pltpu.VMEM((NX, NZ, SHARD, A1 - A0), BF16),
        pltpu.VMEM((NY, NZ, SHARD, B1 - B0), BF16),
        pltpu.VMEM((NY, NX, SHARD, C1 - C0), BF16),
        pltpu.VMEM((NX - 1, NZ, SHARD, A1 - A0), BF16),
        pltpu.VMEM((NY - 1, NZ, SHARD, B1 - B0), BF16),
        pltpu.VMEM((NY * NX, SHARD, C1 - C0), BF16),
        pltpu.VMEM((NZ, SHARD, B1 - A0), BF16),
        pltpu.VMEM((NZ - 1, SHARD, B1 - A0), BF16),
        pltpu.VMEM((ROWS, WIDTH), F32),
        pltpu.VMEM((ROWS, WIDTH), F32),
        pltpu.VMEM((ROWS, WIDTH), F32),
        dma((6,)),
        dma((4,)),
        dma((4,)),
        dma((25,)),
        dma((25,)),
        dma((32,)),
        dma((32,)),
        dma((32,)),
        dma((32,)),
        dma((28,)),
        dma((28,)),
        dma((16,)),
        dma((16,)),
        dma((12,)),
        dma((12,)),
        dma((41,)),
        dma((41,)),
        dma((28,)),
        dma((28,)),
        dma((16,)),
        dma((16,)),
    ]
    return pl.pallas_call(
        kernel,
        out_shape=(pltpu.VMEM((ROWS, WIDTH), BF16), pltpu.VMEM((SHARD, WIDTH), BF16)),
        in_specs=[pl.BlockSpec(memory_space=pl.ANY)] * 6,
        out_specs=(vmem, vmem),
        scratch_shapes=scratch,
        compiler_params=pltpu.CompilerParams(
            collective_id=0, has_side_effects=True, vmem_limit_bytes=56 * 2**20
        ),
        name="contrast",
    )(
        trace_emb,
        code_emb,
        trace_ids.reshape(1, ROWS),
        code_ids.reshape(1, SHARD),
        log_scale.reshape(1, 1),
        bias.reshape(1, 1),
    )


def solution(mesh):
    placed = (
        P(("blk", "group"), None),
        P(("blk", "group"), None),
        P(("blk", "group")),
        P(("blk", "group")),
        P(),
        P(),
    )
    return jax.shard_map(
        per_device,
        mesh=mesh,
        in_specs=placed,
        out_specs=(P(("blk", "group"), None), P(("blk", "group"), None)),
        check_vma=False,
    )
```
